256 devices in a mesh: cam: 8 (over z_lo, core), tile: 32 (over x, z_hi, y).
Axes of the slice: x: 4, y: 4, z: 8 (z_hi: 2, z_lo: 4; z = z_hi * 4 + z_lo), core: 2. Of those that a mesh axis runs over, the one named last changes fastest.
Arguments:
- queries: bfloat16 [8192, 256], P('tile'), as said below
- keys: bfloat16 [16384, 256], P(('cam', 'tile')), as said below
- values: bfloat16 [16384, 256], P(('cam', 'tile')), may hold values from -6 to 6
- grad_out: bfloat16 [8192, 256], P('tile'), may hold values from -6 to 6
- visible: int32 [64, 512], P('tile', 'cam'), may hold values from 0 to 1, as said below
- counts: int32 [512], P('cam'), may hold values from 2 to 32
Outputs:
- grad_queries: bfloat16 [8192, 256], P('tile')
- grad_keys: bfloat16 [16384, 256], P(('cam', 'tile'))
- grad_values: bfloat16 [16384, 256], P(('cam', 'tile'))
The draws below stay inside these ranges and needn't reach their ends.
Inputs may be any that keep to these rules, and one draw needn't show every extreme that they name: Every tile has at least one visible block. `queries`: projected query features. `keys`: projected key features.
All inputs are finite; a program needn't handle non-finite values.
Results may differ from the reference program's by a relative error of at most 0.0052.
Values may be sent and summed in bfloat16 or wider, within the bound.
A program may use at most 128 MiB of HBM per device.

```python
import math
import jax
import jax.numpy as jnp
from jax import lax

C = 256
H = 8
HD = 32
TQ = 128
KB = 32
TILES = 64
QUERIES = 8192
KEYS = 16384
KBLOCKS = 512


def camera_keys(key):
    base = jax.random.fold_in(key, 101)
    return jax.random.normal(base, (KEYS, C), jnp.float32)


def forced_blocks(key):
    return jax.random.randint(jax.random.fold_in(key, 202), (TILES,), 0, KBLOCKS)


def draw_keys(key, part):
    return camera_keys(key).astype(jnp.bfloat16)


def draw_queries(key, part):
    drawn = jax.random.normal(jax.random.fold_in(key, 303), (QUERIES, C), jnp.float32)
    return drawn.astype(jnp.bfloat16)


def draw_visible(key, part):
    coin = jax.random.randint(jax.random.fold_in(key, 404), (TILES, KBLOCKS), 0, 2)
    forced = forced_blocks(key)
    hit = (jnp.arange(KBLOCKS, dtype=jnp.int32)[None, :] == forced[:, None]).astype(jnp.int32)
    return jnp.maximum(coin, hit).astype(jnp.int32)


def plant(values, own_key, least, top_value):
    extent = values.shape
    index_at = [jax.random.randint(jax.random.fold_in(own_key, axis), (), 0, extent[axis]) for axis in range(len(extent))]
    values = values.at[tuple(index_at)].set(least)
    longest = extent.index(max(extent))
    index_at[longest] = (index_at[longest] + 1) % extent[longest]
    return values.at[tuple(index_at)].set(top_value)


def steps_of(own_key, dims, cuts, least, largest):
    def one(dim, parts):
        draws = jax.random.uniform(jax.random.fold_in(jax.random.fold_in(own_key, 6), dim), (parts,), jnp.float32, least / len(cuts), largest / len(cuts))
        return jnp.repeat(jnp.exp(draws), dims[dim] // parts).reshape((-1,) + (1,) * (len(dims) - dim - 1))

    factor_of = one(*cuts[0])
    for cut in cuts[1:]:
        factor_of = factor_of * one(*cut)
    return factor_of


def gaussian(rng, dims, deviation, bound, split=(), held_as=jnp.bfloat16):
    drawn = jax.random.normal(rng, dims, jnp.float32) * deviation
    if len(split) > 0:
        drawn = steps_of(rng, dims, split, -0.22, 0.18) * drawn
    return jnp.clip(drawn, min=-bound, max=bound).astype(held_as)


def setup_inputs(seed: int = 0) -> dict:
    streams_of = jax.random.split(jax.random.key(seed), 7)
    return {
        "queries": draw_queries(jax.random.fold_in(streams_of[6], 71), 0),
        "keys": draw_keys(jax.random.fold_in(streams_of[6], 71), 0),
        "values": gaussian(streams_of[2], (KEYS, C), 1.0, 6.0, ((0, 256),)),
        "grad_out": gaussian(streams_of[3], (QUERIES, C), 1.0, 6.0, ((0, 32),)),
        "visible": draw_visible(jax.random.fold_in(streams_of[6], 71), 0),
        "counts": plant(jax.random.randint(streams_of[5], (KBLOCKS,), 2, KB + 1), jax.random.fold_in(streams_of[5], 1), 2, KB).astype(jnp.int32),
    }


def reference(queries, keys, values, grad_out, visible, counts):
    scale = 1.0 / math.sqrt(HD)
    key_index = jnp.arange(KEYS, dtype=jnp.int32)
    block_of = key_index // KB
    key_valid = key_index % KB < counts[block_of]
    key_heads = keys.astype(jnp.float32).reshape(KEYS, H, HD)
    value_heads = values.astype(jnp.float32).reshape(KEYS, H, HD)

    def tile_step(carry, tile_index):
        grad_k, grad_v = carry
        start = (tile_index * TQ).astype(jnp.int32)
        query_tile = lax.dynamic_slice_in_dim(queries, start, TQ, 0).astype(jnp.float32).reshape(TQ, H, HD)
        grad_tile = lax.dynamic_slice_in_dim(grad_out, start, TQ, 0).astype(jnp.float32).reshape(TQ, H, HD)
        vis_row = lax.dynamic_index_in_dim(visible, tile_index, 0, keepdims=False)
        allowed = ((vis_row[block_of] == 1) & key_valid)[None, None, :]
        scores = jnp.einsum('qhd,khd->hqk', query_tile, key_heads) * scale
        top = lax.optimization_barrier(jnp.max(jnp.where(allowed, scores, -1e+30), axis=-1))
        total = lax.optimization_barrier(jnp.sum(jnp.where(allowed, jnp.exp(scores - top[..., None]), 0.0), axis=-1))
        lse = top + jnp.log(total)
        probs = jnp.where(allowed, jnp.exp(scores - lse[..., None]), 0.0)
        dprobs = jnp.einsum('qhd,khd->hqk', grad_tile, value_heads)
        delta = lax.optimization_barrier(jnp.sum(probs * dprobs, axis=-1))
        dscores = probs * (dprobs - delta[..., None])
        probs_b = probs.astype(jnp.bfloat16).astype(jnp.float32)
        dscores_b = dscores.astype(jnp.bfloat16).astype(jnp.float32)
        grad_q = jnp.einsum('hqk,khd->qhd', dscores_b, key_heads) * scale
        grad_k = grad_k + jnp.einsum('hqk,qhd->khd', dscores_b, query_tile) * scale
        grad_v = grad_v + jnp.einsum('hqk,qhd->khd', probs_b, grad_tile)
        return ((grad_k, grad_v), grad_q.reshape(TQ, C))
    zeros_kv = jnp.zeros((KEYS, H, HD), jnp.float32)
    (grad_k, grad_v), grad_q = lax.scan(tile_step, (zeros_kv, zeros_kv), jnp.arange(TILES, dtype=jnp.int32))
    grad_queries = grad_q.reshape(QUERIES, C).astype(jnp.bfloat16)
    grad_keys = grad_k.reshape(KEYS, C).astype(jnp.bfloat16)
    grad_values = grad_v.reshape(KEYS, C).astype(jnp.bfloat16)
    return (grad_queries, grad_keys, grad_values)
```

```python
import math

import jax
import jax.numpy as jnp
from jax import lax
from jax.experimental import pallas as pl
from jax.experimental.pallas import tpu as pltpu
from jax.sharding import PartitionSpec as P

NX, NY, NZH, NZL, NC = 4, 4, 2, 4, 2
NZ = NZH * NZL
H = 8
HD = 32
C = H * HD
KB = 32
TQ = 128
NEG = -1e30
BIG = 3e38
SCALE = 1.0 / math.sqrt(HD)
LOG2E = math.log2(math.e)
CH = KB * NX
KEYS = 2 * NY * CH
HALF = KEYS // 2
QB = 2 * TQ
QH = QB // NC
QS = QH // NZL

F32 = jnp.float32
BF16 = jnp.bfloat16


def nt(a, b):
    return lax.dot_general(a, b, (((1,), (1,)), ((), ())), preferred_element_type=F32)


def nn(a, b):
    return jnp.dot(a, b, preferred_element_type=F32)


def remote(src, dst, send, recv, device):
    return pltpu.make_async_remote_copy(
        src_ref=src,
        dst_ref=dst,
        send_sem=send,
        recv_sem=recv,
        device_id=device,
        device_id_type=pl.DeviceIdType.MESH,
    )


def kernel(
    q_in, g_in, k_in, v_in, vis_in, cnt_in,
    gq_out, gk_out, gv_out,
    kv, qd, vis, qs, gs, pbuf, dbuf, cap, kt,
    stat, stat_in, core_out, core_in, alpha, delta,
    dk, dv, rs1_out, rs1_in, rs2_own, rs2_out, rs2_in,
    dqt, dq, dq_sib, dqz_own, dqz_out, dqz_in, dqf_out, dqf_in,
    ga1_s, ga1_r, gb1_s, gb1_r, ga2_s, ga2_r, gb2_s, gb2_r,
    qx_s, qx_r, qc_s, qc_r, vx_s, vx_r,
    st_s, st_r, sc_s, sc_r,
    ra1_s, ra1_r, rb1_s, rb1_r, ra2_s, ra2_r, rb2_s, rb2_r,
    dc_s, dc_r, dz_s, dz_r, df_s, df_r,
):
    cam = lax.axis_index("cam")
    tile = lax.axis_index("tile")
    core = lax.rem(cam, NC)
    zl = lax.div(cam, NC)
    y = lax.rem(tile, NY)
    zh = lax.rem(lax.div(tile, NY), NZH)
    x = lax.div(tile, NY * NZH)
    z = zh * NZL + zl

    def at(x_, y_, z_, core_):
        zh_ = lax.div(z_, NZL)
        zl_ = lax.rem(z_, NZL)
        return {"cam": zl_ * NC + core_, "tile": (x_ * NZH + zh_) * NY + y_}

    def xp(j):
        return at(lax.rem(x + j, NX), y, z, core)

    def yp(j):
        return at(x, lax.rem(y + j, NY), z, core)

    def zp(j):
        return at(x, y, lax.rem(z + j, NZ), core)

    def fp(jz, jc):
        return at(x, y, zh * NZL + lax.rem(zl + jz, NZL), lax.rem(core + jc, NC))

    sibling = fp(0, 1)
    mirror = at(x, y, NZ - 1 - z, core)

    barrier = pltpu.get_barrier_semaphore()
    peers = [xp(j) for j in range(1, NX)] + [yp(j) for j in range(1, NY)] + [zp(j) for j in range(1, NZ)]
    peers += [fp(jz, 1) for jz in range(NZL)]
    for peer in peers:
        pl.semaphore_signal(barrier, inc=1, device_id=peer, device_id_type=pl.DeviceIdType.MESH)

    own_a = pl.multiple_of(y * CH + x * KB, KB)
    own_b = pl.multiple_of(HALF + x * CH + y * KB, KB)
    kv[pl.ds(own_a, KB), :C] = k_in[:KB, :]
    kv[pl.ds(own_a, KB), C:] = v_in[:KB, :]
    kv[pl.ds(own_b, KB), :C] = k_in[KB:, :]
    kv[pl.ds(own_b, KB), C:] = v_in[KB:, :]
    qd[zh, 0] = q_in[...]
    qd[zh, 1] = g_in[...]
    vis[zh, :2, : NX * NZH * NY * 2] = vis_in[...].astype(F32)

    pl.semaphore_wait(barrier, len(peers))

    ga1 = [remote(kv.at[pl.ds(own_a, KB)], kv.at[pl.ds(own_a, KB)], ga1_s.at[j - 1], ga1_r.at[j - 1], xp(j)) for j in range(1, NX)]
    gb1 = [remote(kv.at[pl.ds(own_b, KB)], kv.at[pl.ds(own_b, KB)], gb1_s.at[j - 1], gb1_r.at[j - 1], yp(j)) for j in range(1, NY)]
    for copy in ga1 + gb1:
        copy.start()
    qx = remote(qd.at[zh, core], qd.at[zh, core], qx_s.at[0], qx_r.at[0], mirror)
    qx.start()
    vx = remote(vis.at[zh], vis.at[zh], vx_s.at[0], vx_r.at[0], zp(NZL))
    vx.start()

    head_of = lax.broadcasted_iota(jnp.int32, (QB, C), 1) // HD

    def stack(b):
        qb = qd[b, 0]
        gb = qd[b, 1]

        def one(h, _):
            row = pl.multiple_of((b * H + h) * QB, QB)
            keep = head_of == h
            qs[pl.ds(row, QB), :] = jnp.where(keep, qb, jnp.zeros_like(qb))
            gs[pl.ds(row, QB), :] = jnp.where(keep, gb, jnp.zeros_like(gb))
            return 0

        lax.fori_loop(0, H, one, 0)

    stack(zh)

    chunk_a = pl.multiple_of(y * CH, CH)
    chunk_b = pl.multiple_of(HALF + x * CH, CH)
    for copy in ga1 + gb1:
        copy.wait_recv()
    ga2 = [remote(kv.at[pl.ds(chunk_a, CH)], kv.at[pl.ds(chunk_a, CH)], ga2_s.at[j - 1], ga2_r.at[j - 1], yp(j)) for j in range(1, NY)]
    gb2 = [remote(kv.at[pl.ds(chunk_b, CH)], kv.at[pl.ds(chunk_b, CH)], gb2_s.at[j - 1], gb2_r.at[j - 1], xp(j)) for j in range(1, NX)]
    for copy in ga2 + gb2:
        copy.start()

    blocks = NX * NZH * NY * 2
    row = lax.broadcasted_iota(jnp.int32, (KEYS, blocks), 0)
    col = lax.broadcasted_iota(jnp.int32, (KEYS, blocks), 1)
    half = row // HALF
    outer = (row % HALF) // CH
    inner = (row % CH) // KB
    bx = jnp.where(half == 0, inner, outer)
    by = jnp.where(half == 0, outer, inner)
    block = 2 * ((bx * NZH + zh) * NY + by) + half
    pick = ((block == col) & (row % KB < cnt_in[...])).astype(F32).astype(BF16)
    vx.wait_recv()
    for b in range(NZH):
        seen = jnp.concatenate(
            [jnp.broadcast_to(vis[b, t : t + 1, :blocks], (TQ, blocks)) for t in range(2)], axis=0
        ).astype(BF16)
        cap[b] = jnp.where(nt(pick, seen) > 0.5, BIG, NEG)

    qx.wait_recv()
    qc = remote(qd.at[1 - zh, core], qd.at[1 - zh, core], qc_s.at[0], qc_r.at[0], sibling)
    qc.start()
    for copy in ga2 + gb2:
        copy.wait_recv()
    kt[...] = kv[:, :C].astype(F32).T.astype(BF16)
    qc.wait_recv()
    stack(1 - zh)

    def first(b, lo, hi):
        def one(h, _):
            i = b * H + h
            rows = pl.ds(pl.multiple_of(i * QB, QB), QB)
            s = nt(kv[:, :C], qs[rows, :]) * (SCALE * LOG2E)
            s = jnp.minimum(s, cap[b])
            m = jnp.maximum(jnp.max(s, axis=0, keepdims=True), 0.1 * NEG)
            p = jnp.exp2(s - m)
            pbuf[i] = p
            d = nt(kv[:, C:], gs[rows, :])
            dbuf[i] = d
            stat[b, 0, pl.ds(h, 1), :] = m
            stat[b, 1, pl.ds(h, 1), :] = jnp.sum(p, axis=0, keepdims=True)
            stat[b, 2, pl.ds(h, 1), :] = jnp.sum(p * d, axis=0, keepdims=True)
            return 0

        lax.fori_loop(lo, hi, one, 0)

    def stat_copies(b):
        return [remote(stat.at[b], stat_in.at[b, j - 1], st_s.at[b, j - 1], st_r.at[b, j - 1], zp(j)) for j in range(1, NZ)]

    def core_copy(b):
        return remote(core_out.at[b], core_in.at[b], sc_s.at[b], sc_r.at[b], sibling)

    def merge(parts):
        top = parts[0][0]
        for part in parts[1:]:
            top = jnp.maximum(top, part[0])
        total = jnp.zeros_like(top)
        dot = jnp.zeros_like(top)
        for m, l, d in parts:
            w = jnp.exp2(m - top)
            total = total + l * w
            dot = dot + d * w
        return top, total, dot

    def stat_ring(b):
        for copy in stat_copies(b):
            copy.wait_recv()
        parts = [tuple(stat[b, k] for k in range(3))]
        parts += [tuple(stat_in[b, j, k] for k in range(3)) for j in range(NZ - 1)]
        for k, value in enumerate(merge(parts)):
            core_out[b, k] = value
        core_copy(b).start()

    def stat_final(b):
        core_copy(b).wait_recv()
        top, total, dot = merge([tuple(core_out[b, k] for k in range(3)), tuple(core_in[b, k] for k in range(3))])
        inv = 1.0 / total
        alpha[b] = jnp.exp2(stat[b, 0] - top) * inv
        delta[b] = dot * inv

    def chunk_copies(i):
        return (
            remote(rs1_out.at[i, 0], rs1_in.at[i, 0], ra1_s.at[i], ra1_r.at[i], yp(i + 1)),
            remote(rs1_out.at[i, 1], rs1_in.at[i, 1], rb1_s.at[i], rb1_r.at[i], xp(i + 1)),
        )

    def second(b, lo, hi):
        stack_rows = pl.ds(b * H * QB, H * QB)

        def one(i, _):
            ra = pl.ds(pl.multiple_of(lax.rem(y + 1 + i, NY) * CH, CH), CH)
            rb = pl.ds(pl.multiple_of(HALF + lax.rem(x + 1 + i, NX) * CH, CH), CH)
            ps = []
            ts = []
            dqs = []
            ktc = jnp.concatenate([kt[:, ra], kt[:, rb]], axis=1)
            for h in range(H):
                n = b * H + h
                a = alpha[b, h : h + 1, :]
                e = delta[b, h : h + 1, :]
                p = jnp.concatenate([pbuf[n, ra, :], pbuf[n, rb, :]], axis=0) * a
                d = jnp.concatenate([dbuf[n, ra, :], dbuf[n, rb, :]], axis=0)
                t = (p * (d - e)).astype(BF16)
                ps.append(p.astype(BF16))
                ts.append(t)
                dqs.append(nn(ktc[h * HD : (h + 1) * HD, :], t))
            dqc = jnp.concatenate(dqs, axis=0)
            dkc = nn(jnp.concatenate(ts, axis=1), qs[stack_rows, :])
            dvc = nn(jnp.concatenate(ps, axis=1), gs[stack_rows, :])
            if b == 0:
                dk[i] = dkc
                dv[i] = dvc
            else:
                dkc = dk[i] + dkc
                dvc = dv[i] + dvc

                @pl.when(i < NX - 1)
                def _():
                    rs1_out[i, 0, :, :C] = dkc[:CH].astype(BF16)
                    rs1_out[i, 1, :, :C] = dkc[CH:].astype(BF16)
                    rs1_out[i, 0, :, C:] = dvc[:CH].astype(BF16)
                    rs1_out[i, 1, :, C:] = dvc[CH:].astype(BF16)
                    for copy in chunk_copies(i):
                        copy.start()

                @pl.when(i == NX - 1)
                def _():
                    dk[i] = dkc
                    dv[i] = dvc

            @pl.when(i == 0)
            def _():
                dqt[b] = dqc

            @pl.when(i > 0)
            def _():
                dqt[b] = dqt[b] + dqc

            return 0

        lax.fori_loop(lo, hi, one, 0)

    other_half = pl.ds(pl.multiple_of((1 - core) * QH, QH), QH)

    def dq_core(b):
        return remote(dq.at[b, other_half], dq_sib.at[b], dc_s.at[b], dc_r.at[b], sibling)

    def dq_start(b):
        dq[b] = dqt[b].T * SCALE
        dq_core(b).start()

    def dq_slot(b, j):
        return remote(
            dqz_out.at[b, pl.ds(j * QS, QS)],
            dqz_in.at[z],
            dz_s.at[b * NZL + j],
            dz_r.at[z],
            at(x, y, b * NZL + j, core),
        )

    def dq_ring(b):
        dq_core(b).wait_recv()
        mine = dq[b, pl.ds(pl.multiple_of(core * QH, QH), QH), :] + dq_sib[b]
        dqz_out[b] = mine.astype(BF16)
        for j in range(NZL):

            @pl.when(z == b * NZL + j)
            def _(j=j):
                dqz_own[...] = mine[j * QS : (j + 1) * QS, :]

            @pl.when(z != b * NZL + j)
            def _(j=j):
                dq_slot(b, j).start()

    first(0, 0, H)
    for copy in stat_copies(0):
        copy.start()
    first(1, 0, H // 2)
    stat_ring(0)
    first(1, H // 2, H)
    for copy in stat_copies(1):
        copy.start()
    stat_final(0)
    second(0, 0, NX // 2)
    stat_ring(1)
    second(0, NX // 2, NX)
    dq_start(0)
    stat_final(1)
    second(1, 0, NX // 2)
    dq_ring(0)
    second(1, NX // 2, NX)
    dq_start(1)

    for i in range(NX - 1):
        for copy in chunk_copies(i):
            copy.wait_recv()
    for half in range(2):
        for part, acc in enumerate((dk, dv)):
            cols = slice(part * C, (part + 1) * C)
            total = acc[NX - 1, half * CH : (half + 1) * CH, :]
            for i in range(NX - 1):
                total = total + rs1_in[i, half, :, cols].astype(F32)
            rs2_own[half, :, cols] = total
            rs2_out[half, :, cols] = total.astype(BF16)

    def rs2_copies(j):
        rows_a = pl.ds(pl.multiple_of(lax.rem(x + j, NX) * KB, KB), KB)
        rows_b = pl.ds(pl.multiple_of(lax.rem(y + j, NY) * KB, KB), KB)
        return (
            remote(rs2_out.at[0, rows_a], rs2_in.at[j - 1, 0], ra2_s.at[j - 1], ra2_r.at[j - 1], xp(j)),
            remote(rs2_out.at[1, rows_b], rs2_in.at[j - 1, 1], rb2_s.at[j - 1], rb2_r.at[j - 1], yp(j)),
        )

    for j in range(1, NX):
        for copy in rs2_copies(j):
            copy.start()

    dq_ring(1)
    total = dqz_own[...]
    for j in range(1, NZ):
        sender = lax.rem(z + j, NZ)
        remote(dqz_out.at[0, pl.ds(0, QS)], dqz_in.at[sender], dz_s.at[0], dz_r.at[sender], sibling).wait_recv()
        total = total + dqz_in[sender].astype(F32)
    dqf_out[...] = total.astype(BF16)

    def dqf_copy(jz, jc):
        k = jz * NC + jc - 1
        return remote(dqf_out, dqf_in.at[k], df_s.at[k], df_r.at[k], fp(jz, jc))

    others = [(jz, jc) for jz in range(NZL) for jc in range(NC) if jz + jc > 0]
    for jz, jc in others:
        dqf_copy(jz, jc).start()
    gq_out[pl.ds(pl.multiple_of(core * QH + zl * QS, QS), QS), :] = dqf_out[...]

    for j in range(1, NX):
        for copy in rs2_copies(j):
            copy.wait_recv()
    for half, pos in ((0, x), (1, y)):
        rows = pl.ds(pl.multiple_of(pos * KB, KB), KB)
        total = rs2_own[half, rows, :]
        for j in range(NX - 1):
            total = total + rs2_in[j, half].astype(F32)
        gk_out[half * KB : (half + 1) * KB, :] = (total[:, :C] * SCALE).astype(BF16)
        gv_out[half * KB : (half + 1) * KB, :] = total[:, C:].astype(BF16)

    for jz, jc in others:
        dqf_copy(jz, jc).wait_recv()
        fz = lax.rem(zl - jz + NZL, NZL)
        fc = lax.rem(core - jc + NC, NC)
        gq_out[pl.ds(pl.multiple_of(fc * QH + fz * QS, QS), QS), :] = dqf_in[jz * NC + jc - 1]

    for copy in ga1 + gb1 + ga2 + gb2 + [qx, vx, qc]:
        copy.wait_send()
    for b in range(NZH):
        for copy in stat_copies(b):
            copy.wait_send()
        core_copy(b).wait_send()
        dq_core(b).wait_send()
        for j in range(NZL):

            @pl.when(z != b * NZL + j)
            def _(b=b, j=j):
                dq_slot(b, j).wait_send()

    for i in range(NX - 1):
        for copy in chunk_copies(i):
            copy.wait_send()
    for j in range(1, NX):
        for copy in rs2_copies(j):
            copy.wait_send()
    for jz, jc in others:
        dqf_copy(jz, jc).wait_send()


def shards(queries, keys, values, grad_out, visible, counts):
    vmem = pl.BlockSpec(memory_space=pltpu.VMEM)
    dma = pltpu.SemaphoreType.DMA
    V = pltpu.VMEM
    scratch = [
        V((KEYS, 2 * C), BF16),
        V((NZH, 2, QB, C), BF16),
        V((NZH, 8, 128), F32),
        V((NZH * H * QB, C), BF16),
        V((NZH * H * QB, C), BF16),
        V((NZH * H, KEYS, QB), F32),
        V((NZH * H, KEYS, QB), F32),
        V((NZH, KEYS, QB), F32),
        V((C, KEYS), BF16),
        V((NZH, 3, H, QB), F32),
        V((NZH, NZ - 1, 3, H, QB), F32),
        V((NZH, 3, H, QB), F32),
        V((NZH, 3, H, QB), F32),
        V((NZH, H, QB), F32),
        V((NZH, H, QB), F32),
        V((NX, 2 * CH, C), F32),
        V((NX, 2 * CH, C), F32),
        V((NX - 1, 2, CH, 2 * C), BF16),
        V((NX - 1, 2, CH, 2 * C), BF16),
        V((2, CH, 2 * C), F32),
        V((2, CH, 2 * C), BF16),
        V((NX - 1, 2, KB, 2 * C), BF16),
        V((NZH, C, QB), F32),
        V((NZH, QB, C), F32),
        V((NZH, QH, C), F32),
        V((QS, C), F32),
        V((NZH, QH, C), BF16),
        V((NZ, QS, C), BF16),
        V((QS, C), BF16),
        V((NZL * NC - 1, QS, C), BF16),
    ]
    sems = [(NX - 1,)] * 8 + [(1,)] * 6 + [(NZH, NZ - 1)] * 2 + [(NZH,)] * 2 + [(NX - 1,)] * 8
    sems += [(NZH,)] * 2 + [(NZ,)] * 2 + [(NZL * NC - 1,)] * 2
    scratch += [dma(s) for s in sems]
    return pl.pallas_call(
        kernel,
        out_shape=(
            jax.ShapeDtypeStruct((QB, C), BF16),
            jax.ShapeDtypeStruct((2 * KB, C), BF16),
            jax.ShapeDtypeStruct((2 * KB, C), BF16),
        ),
        in_specs=[vmem] * 6,
        out_specs=(vmem,) * 3,
        scratch_shapes=scratch,
        compiler_params=pltpu.CompilerParams(
            collective_id=0, has_side_effects=True, vmem_limit_bytes=60 * 1024 * 1024
        ),
    )(queries, grad_out, keys, values, visible, counts.reshape(1, -1))


def solution(mesh):
    in_specs = (
        P("tile", None),
        P(("cam", "tile"), None),
        P(("cam", "tile"), None),
        P("tile", None),
        P("tile", "cam"),
        P("cam"),
    )
    out_specs = (P("tile", None), P(("cam", "tile"), None), P(("cam", "tile"), None))
    return jax.shard_map(shards, mesh=mesh, in_specs=in_specs, out_specs=out_specs, check_vma=False)
```

```python
import math

import jax
import jax.numpy as jnp
from jax import lax
from jax.experimental import pallas as pl
from jax.experimental.pallas import tpu as pltpu
from jax.sharding import PartitionSpec as P

NX, NY, NZH, NZL, NC = 4, 4, 2, 4, 2
NZ = NZH * NZL
H = 8
HD = 32
C = H * HD
KB = 32
TQ = 128
NEG = -1e30
BIG = 3e38
SCALE = 1.0 / math.sqrt(HD)
LOG2E = math.log2(math.e)
CH = KB * NX
KEYS = 2 * NY * CH
HALF = KEYS // 2
QB = 2 * TQ
QH = QB // NC
QS = QH // NZL

F32 = jnp.float32
BF16 = jnp.bfloat16


def nt(a, b):
    return lax.dot_general(a, b, (((1,), (1,)), ((), ())), preferred_element_type=F32)


def nn(a, b):
    return jnp.dot(a, b, preferred_element_type=F32)


def remote(src, dst, send, recv, device):
    return pltpu.make_async_remote_copy(
        src_ref=src,
        dst_ref=dst,
        send_sem=send,
        recv_sem=recv,
        device_id=device,
        device_id_type=pl.DeviceIdType.MESH,
    )


def kernel(
    q_in, g_in, k_in, v_in, vis_in, cnt_in,
    gq_out, gk_out, gv_out,
    kv, qd, vis, qs, gs, pbuf, dbuf, cap, kt,
    cstat, stat, stat_in, core_out, core_in, alpha, delta,
    dk, dv, rs1_out, rs1_in, rs2_own, rs2_out, rs2_in,
    dqt, dq, dq_sib, dqz_own, dqz_out, dqz_in, dqf_out, dqf_in,
    ga1_s, ga1_r, gb1_s, gb1_r, ga2_s, ga2_r, gb2_s, gb2_r,
    qx_s, qx_r, qc_s, qc_r, vx_s, vx_r,
    st_s, st_r, sc_s, sc_r,
    ra1_s, ra1_r, rb1_s, rb1_r, ra2_s, ra2_r, rb2_s, rb2_r,
    dc_s, dc_r, dz_s, dz_r, df_s, df_r,
):
    cam = lax.axis_index("cam")
    tile = lax.axis_index("tile")
    core = lax.rem(cam, NC)
    zl = lax.div(cam, NC)
    y = lax.rem(tile, NY)
    zh = lax.rem(lax.div(tile, NY), NZH)
    x = lax.div(tile, NY * NZH)
    z = zh * NZL + zl

    def at(x_, y_, z_, core_):
        zh_ = lax.div(z_, NZL)
        zl_ = lax.rem(z_, NZL)
        return {"cam": zl_ * NC + core_, "tile": (x_ * NZH + zh_) * NY + y_}

    def xp(j):
        return at(lax.rem(x + j, NX), y, z, core)

    def yp(j):
        return at(x, lax.rem(y + j, NY), z, core)

    def zp(j):
        return at(x, y, lax.rem(z + j, NZ), core)

    def fp(jz, jc):
        return at(x, y, zh * NZL + lax.rem(zl + jz, NZL), lax.rem(core + jc, NC))

    sibling = fp(0, 1)
    mirror = at(x, y, NZ - 1 - z, core)

    barrier = pltpu.get_barrier_semaphore()
    peers = [xp(j) for j in range(1, NX)] + [yp(j) for j in range(1, NY)] + [zp(j) for j in range(1, NZ)]
    peers += [fp(jz, 1) for jz in range(NZL)]
    for peer in peers:
        pl.semaphore_signal(barrier, inc=1, device_id=peer, device_id_type=pl.DeviceIdType.MESH)

    own_a = pl.multiple_of(y * CH + x * KB, KB)
    own_b = pl.multiple_of(HALF + x * CH + y * KB, KB)
    kv[pl.ds(own_a, KB), :C] = k_in[:KB, :]
    kv[pl.ds(own_a, KB), C:] = v_in[:KB, :]
    kv[pl.ds(own_b, KB), :C] = k_in[KB:, :]
    kv[pl.ds(own_b, KB), C:] = v_in[KB:, :]
    qd[zh, 0] = q_in[...]
    qd[zh, 1] = g_in[...]
    vis[zh, :2, : NX * NZH * NY * 2] = vis_in[...].astype(F32)

    pl.semaphore_wait(barrier, len(peers))

    ga1 = [remote(kv.at[pl.ds(own_a, KB)], kv.at[pl.ds(own_a, KB)], ga1_s.at[j - 1], ga1_r.at[j - 1], xp(j)) for j in range(1, NX)]
    gb1 = [remote(kv.at[pl.ds(own_b, KB)], kv.at[pl.ds(own_b, KB)], gb1_s.at[j - 1], gb1_r.at[j - 1], yp(j)) for j in range(1, NY)]
    for copy in ga1 + gb1:
        copy.start()
    qx = remote(qd.at[zh, core], qd.at[zh, core], qx_s.at[0], qx_r.at[0], mirror)
    qx.start()
    vx = remote(vis.at[zh], vis.at[zh], vx_s.at[0], vx_r.at[0], zp(NZL))
    vx.start()

    head_of = lax.broadcasted_iota(jnp.int32, (QB, C), 1) // HD

    def stack(b):
        qb = qd[b, 0]
        gb = qd[b, 1]

        def one(h, _):
            row = pl.multiple_of((b * H + h) * QB, QB)
            keep = head_of == h
            qs[pl.ds(row, QB), :] = jnp.where(keep, qb, jnp.zeros_like(qb))
            gs[pl.ds(row, QB), :] = jnp.where(keep, gb, jnp.zeros_like(gb))
            return 0

        lax.fori_loop(0, H, one, 0)

    stack(zh)

    blocks = NX * NZH * NY * 2
    row = lax.broadcasted_iota(jnp.int32, (KEYS, blocks), 0)
    col = lax.broadcasted_iota(jnp.int32, (KEYS, blocks), 1)
    half = row // HALF
    outer = (row % HALF) // CH
    inner = (row % CH) // KB
    bx = jnp.where(half == 0, inner, outer)
    by = jnp.where(half == 0, outer, inner)
    block = 2 * ((bx * NZH + zh) * NY + by) + half
    pick = ((block == col) & (row % KB < cnt_in[...])).astype(F32).astype(BF16)

    def cap_of(b):
        seen = jnp.concatenate(
            [jnp.broadcast_to(vis[b, t : t + 1, :blocks], (TQ, blocks)) for t in range(2)], axis=0
        ).astype(BF16)
        cap[b] = jnp.where(nt(pick, seen) > 0.5, BIG, NEG)

    cap_of(zh)

    chunk_a = pl.multiple_of(y * CH, CH)
    chunk_b = pl.multiple_of(HALF + x * CH, CH)
    for copy in ga1 + gb1:
        copy.wait_recv()
    ga2 = [remote(kv.at[pl.ds(chunk_a, CH)], kv.at[pl.ds(chunk_a, CH)], ga2_s.at[j - 1], ga2_r.at[j - 1], yp(j)) for j in range(1, NY)]
    gb2 = [remote(kv.at[pl.ds(chunk_b, CH)], kv.at[pl.ds(chunk_b, CH)], gb2_s.at[j - 1], gb2_r.at[j - 1], xp(j)) for j in range(1, NX)]
    for j in (0, 2, 1):
        ga2[j].start()
        gb2[j].start()

    def chunk_rows(i):
        ra = pl.ds(pl.multiple_of(lax.rem(y + 1 + i, NY) * CH, CH), CH)
        rb = pl.ds(pl.multiple_of(HALF + lax.rem(x + 1 + i, NX) * CH, CH), CH)
        return ra, rb

    def first(b, i):
        ra, rb = chunk_rows(i)
        kc = jnp.concatenate([kv[ra, :C], kv[rb, :C]], axis=0)
        vc = jnp.concatenate([kv[ra, C:], kv[rb, C:]], axis=0)
        n = b * NX + i
        for h in range(H):
            rows = pl.ds(pl.multiple_of((b * H + h) * QB, QB), QB)
            s = nt(kc, qs[rows, :]) * (SCALE * LOG2E)
            s = jnp.minimum(s, jnp.concatenate([cap[b, ra, :], cap[b, rb, :]], axis=0))
            m = jnp.maximum(jnp.max(s, axis=0, keepdims=True), 0.1 * NEG)
            p = jnp.exp2(s - m)
            pbuf[n, h] = p
            d = nt(vc, gs[rows, :])
            dbuf[n, h] = d
            cstat[n, 0, h : h + 1, :] = m
            cstat[n, 1, h : h + 1, :] = jnp.sum(p, axis=0, keepdims=True)
            cstat[n, 2, h : h + 1, :] = jnp.sum(p * d, axis=0, keepdims=True)

    def stat_copies(b):
        return [remote(stat.at[b], stat_in.at[b, j - 1], st_s.at[b, j - 1], st_r.at[b, j - 1], zp(j)) for j in range(1, NZ)]

    def stat_send(b):
        parts = [tuple(cstat[b * NX + i, k] for k in range(3)) for i in range(NX)]
        top = parts[0][0]
        for part in parts[1:]:
            top = jnp.maximum(top, part[0])
        total = jnp.zeros_like(top)
        dot = jnp.zeros_like(top)
        for m, l, d in parts:
            w = jnp.exp2(m - top)
            total = total + l * w
            dot = dot + d * w
        total = jnp.maximum(total, 1e-30)
        stat[b, 0] = top + jnp.log2(total)
        stat[b, 1] = dot / total
        for copy in stat_copies(b):
            copy.start()

    def core_copy(b):
        return remote(core_out.at[b], core_in.at[b], sc_s.at[b], sc_r.at[b], sibling)

    def merge(parts):
        top = parts[0][0]
        for part in parts[1:]:
            top = jnp.maximum(top, part[0])
        total = jnp.zeros_like(top)
        dot = jnp.zeros_like(top)
        for lse, mean in parts:
            w = jnp.exp2(lse - top)
            total = total + w
            dot = dot + mean * w
        return top + jnp.log2(total), dot / total

    def stat_ring(b):
        for copy in stat_copies(b):
            copy.wait_recv()
        parts = [(stat[b, 0], stat[b, 1])]
        parts += [(stat_in[b, j, 0], stat_in[b, j, 1]) for j in range(NZ - 1)]
        for k, value in enumerate(merge(parts)):
            core_out[b, k] = value
        core_copy(b).start()

    def stat_final(b):
        core_copy(b).wait_recv()
        lse, mean = merge([(core_out[b, 0], core_out[b, 1]), (core_in[b, 0], core_in[b, 1])])
        for i in range(NX):
            alpha[b * NX + i] = jnp.exp2(cstat[b * NX + i, 0] - lse)
        delta[b] = mean

    def chunk_copies(i):
        return (
            remote(rs1_out.at[i, 0], rs1_in.at[i, 0], ra1_s.at[i], ra1_r.at[i], yp(i + 1)),
            remote(rs1_out.at[i, 1], rs1_in.at[i, 1], rb1_s.at[i], rb1_r.at[i], xp(i + 1)),
        )

    def second(b, lo, hi):
        stack_rows = pl.ds(b * H * QB, H * QB)

        def one(i, _):
            n = b * NX + i
            ps = []
            ts = []
            dqs = []
            for h in range(H):
                a = alpha[n, h : h + 1, :]
                e = delta[b, h : h + 1, :]
                p = pbuf[n, h] * a
                d = dbuf[n, h]
                t = (p * (d - e)).astype(BF16)
                ps.append(p.astype(BF16))
                ts.append(t)
                dqs.append(nn(kt[i, h * HD : (h + 1) * HD, :], t))
            dqc = jnp.concatenate(dqs, axis=0)
            dkc = nn(jnp.concatenate(ts, axis=1), qs[stack_rows, :])
            dvc = nn(jnp.concatenate(ps, axis=1), gs[stack_rows, :])
            if b == 0:
                dk[i] = dkc
                dv[i] = dvc
            else:
                dkc = dk[i] + dkc
                dvc = dv[i] + dvc

                @pl.when(i < NX - 1)
                def _():
                    rs1_out[i, 0, :, :C] = dkc[:CH].astype(BF16)
                    rs1_out[i, 1, :, :C] = dkc[CH:].astype(BF16)
                    rs1_out[i, 0, :, C:] = dvc[:CH].astype(BF16)
                    rs1_out[i, 1, :, C:] = dvc[CH:].astype(BF16)
                    for copy in chunk_copies(i):
                        copy.start()

                @pl.when(i == NX - 1)
                def _():
                    dk[i] = dkc
                    dv[i] = dvc

            @pl.when(i == 0)
            def _():
                dqt[b] = dqc

            @pl.when(i > 0)
            def _():
                dqt[b] = dqt[b] + dqc

            return 0

        lax.fori_loop(lo, hi, one, 0)

    other_half = pl.ds(pl.multiple_of((1 - core) * QH, QH), QH)

    def dq_core(b):
        return remote(dq.at[b, other_half], dq_sib.at[b], dc_s.at[b], dc_r.at[b], sibling)

    def dq_start(b):
        dq[b] = dqt[b].T * SCALE
        dq_core(b).start()

    def dq_slot(b, j):
        return remote(
            dqz_out.at[b, pl.ds(j * QS, QS)],
            dqz_in.at[z],
            dz_s.at[b * NZL + j],
            dz_r.at[z],
            at(x, y, b * NZL + j, core),
        )

    def dq_ring(b):
        dq_core(b).wait_recv()
        mine = dq[b, pl.ds(pl.multiple_of(core * QH, QH), QH), :] + dq_sib[b]
        dqz_out[b] = mine.astype(BF16)
        for j in range(NZL):

            @pl.when(z == b * NZL + j)
            def _(j=j):
                dqz_own[...] = mine[j * QS : (j + 1) * QS, :]

            @pl.when(z != b * NZL + j)
            def _(j=j):
                dq_slot(b, j).start()

    first(zh, NX - 1)
    vx.wait_recv()
    cap_of(1 - zh)
    qx.wait_recv()
    qc = remote(qd.at[1 - zh, core], qd.at[1 - zh, core], qc_s.at[0], qc_r.at[0], sibling)
    qc.start()
    qc.wait_recv()
    stack(1 - zh)

    def unit(n, _):
        for step, j in enumerate((2, 0, 1)):

            @pl.when(n == step)
            def _(j=j):
                ga2[j].wait_recv()
                gb2[j].wait_recv()

        in_0 = NX - 1 + zh
        b = (n >= in_0).astype(jnp.int32)
        place = jnp.where(b == 0, n + 1 - zh, n - in_0 + zh)
        i = jnp.where(place == 0, NX - 1, jnp.where(place == 1, 0, jnp.where(place == 2, 2, 1)))
        first(b, i)

        @pl.when(n == in_0 - 1)
        def _():
            stat_send(0)

        return 0

    lax.fori_loop(0, NZH * NX - 1, unit, 0)
    stat_send(1)
    for i in range(NX):
        ra, rb = chunk_rows(i)
        kt[i] = jnp.concatenate([kv[ra, :C], kv[rb, :C]], axis=0).astype(F32).T.astype(BF16)
    stat_ring(0)
    stat_final(0)
    second(0, 0, NX // 2)
    stat_ring(1)
    second(0, NX // 2, NX)
    dq_start(0)
    stat_final(1)
    second(1, 0, NX // 2)
    dq_ring(0)
    second(1, NX // 2, NX)
    dq_start(1)

    for i in range(NX - 1):
        for copy in chunk_copies(i):
            copy.wait_recv()
    for half in range(2):
        for part, acc in enumerate((dk, dv)):
            cols = slice(part * C, (part + 1) * C)
            total = acc[NX - 1, half * CH : (half + 1) * CH, :]
            for i in range(NX - 1):
                total = total + rs1_in[i, half, :, cols].astype(F32)
            rs2_own[half, :, cols] = total
            rs2_out[half, :, cols] = total.astype(BF16)

    def rs2_copies(j):
        rows_a = pl.ds(pl.multiple_of(lax.rem(x + j, NX) * KB, KB), KB)
        rows_b = pl.ds(pl.multiple_of(lax.rem(y + j, NY) * KB, KB), KB)
        return (
            remote(rs2_out.at[0, rows_a], rs2_in.at[j - 1, 0], ra2_s.at[j - 1], ra2_r.at[j - 1], xp(j)),
            remote(rs2_out.at[1, rows_b], rs2_in.at[j - 1, 1], rb2_s.at[j - 1], rb2_r.at[j - 1], yp(j)),
        )

    for j in range(1, NX):
        for copy in rs2_copies(j):
            copy.start()

    dq_ring(1)
    total = dqz_own[...]
    for j in range(1, NZ):
        sender = lax.rem(z + j, NZ)
        remote(dqz_out.at[0, pl.ds(0, QS)], dqz_in.at[sender], dz_s.at[0], dz_r.at[sender], sibling).wait_recv()
        total = total + dqz_in[sender].astype(F32)
    dqf_out[...] = total.astype(BF16)

    def dqf_copy(jz, jc):
        k = jz * NC + jc - 1
        return remote(dqf_out, dqf_in.at[k], df_s.at[k], df_r.at[k], fp(jz, jc))

    others = [(jz, jc) for jz in range(NZL) for jc in range(NC) if jz + jc > 0]
    for jz, jc in others:
        dqf_copy(jz, jc).start()
    gq_out[pl.ds(pl.multiple_of(core * QH + zl * QS, QS), QS), :] = dqf_out[...]

    for j in range(1, NX):
        for copy in rs2_copies(j):
            copy.wait_recv()
    for half, pos in ((0, x), (1, y)):
        rows = pl.ds(pl.multiple_of(pos * KB, KB), KB)
        total = rs2_own[half, rows, :]
        for j in range(NX - 1):
            total = total + rs2_in[j, half].astype(F32)
        gk_out[half * KB : (half + 1) * KB, :] = (total[:, :C] * SCALE).astype(BF16)
        gv_out[half * KB : (half + 1) * KB, :] = total[:, C:].astype(BF16)

    for jz, jc in others:
        dqf_copy(jz, jc).wait_recv()
        fz = lax.rem(zl - jz + NZL, NZL)
        fc = lax.rem(core - jc + NC, NC)
        gq_out[pl.ds(pl.multiple_of(fc * QH + fz * QS, QS), QS), :] = dqf_in[jz * NC + jc - 1]

    for copy in ga1 + gb1 + ga2 + gb2 + [qx, vx, qc]:
        copy.wait_send()
    for b in range(NZH):
        for copy in stat_copies(b):
            copy.wait_send()
        core_copy(b).wait_send()
        dq_core(b).wait_send()
        for j in range(NZL):

            @pl.when(z != b * NZL + j)
            def _(b=b, j=j):
                dq_slot(b, j).wait_send()

    for i in range(NX - 1):
        for copy in chunk_copies(i):
            copy.wait_send()
    for j in range(1, NX):
        for copy in rs2_copies(j):
            copy.wait_send()
    for jz, jc in others:
        dqf_copy(jz, jc).wait_send()


def shards(queries, keys, values, grad_out, visible, counts):
    vmem = pl.BlockSpec(memory_space=pltpu.VMEM)
    dma = pltpu.SemaphoreType.DMA
    V = pltpu.VMEM
    scratch = [
        V((KEYS, 2 * C), BF16),
        V((NZH, 2, QB, C), BF16),
        V((NZH, 8, 128), F32),
        V((NZH * H * QB, C), BF16),
        V((NZH * H * QB, C), BF16),
        V((NZH * NX, H, 2 * CH, QB), F32),
        V((NZH * NX, H, 2 * CH, QB), F32),
        V((NZH, KEYS, QB), F32),
        V((NX, C, 2 * CH), BF16),
        V((NZH * NX, 3, H, QB), F32),
        V((NZH, 2, H, QB), F32),
        V((NZH, NZ - 1, 2, H, QB), F32),
        V((NZH, 2, H, QB), F32),
        V((NZH, 2, H, QB), F32),
        V((NZH * NX, H, QB), F32),
        V((NZH, H, QB), F32),
        V((NX, 2 * CH, C), F32),
        V((NX, 2 * CH, C), F32),
        V((NX - 1, 2, CH, 2 * C), BF16),
        V((NX - 1, 2, CH, 2 * C), BF16),
        V((2, CH, 2 * C), F32),
        V((2, CH, 2 * C), BF16),
        V((NX - 1, 2, KB, 2 * C), BF16),
        V((NZH, C, QB), F32),
        V((NZH, QB, C), F32),
        V((NZH, QH, C), F32),
        V((QS, C), F32),
        V((NZH, QH, C), BF16),
        V((NZ, QS, C), BF16),
        V((QS, C), BF16),
        V((NZL * NC - 1, QS, C), BF16),
    ]
    sems = [(NX - 1,)] * 8 + [(1,)] * 6 + [(NZH, NZ - 1)] * 2 + [(NZH,)] * 2 + [(NX - 1,)] * 8
    sems += [(NZH,)] * 2 + [(NZ,)] * 2 + [(NZL * NC - 1,)] * 2
    scratch += [dma(s) for s in sems]
    return pl.pallas_call(
        kernel,
        out_shape=(
            jax.ShapeDtypeStruct((QB, C), BF16),
            jax.ShapeDtypeStruct((2 * KB, C), BF16),
            jax.ShapeDtypeStruct((2 * KB, C), BF16),
        ),
        in_specs=[vmem] * 6,
        out_specs=(vmem,) * 3,
        scratch_shapes=scratch,
        compiler_params=pltpu.CompilerParams(
            collective_id=0, has_side_effects=True, vmem_limit_bytes=60 * 1024 * 1024
        ),
    )(queries, grad_out, keys, values, visible, counts.reshape(1, -1))


def solution(mesh):
    in_specs = (
        P("tile", None),
        P(("cam", "tile"), None),
        P(("cam", "tile"), None),
        P("tile", None),
        P("tile", "cam"),
        P("cam"),
    )
    out_specs = (P("tile", None), P(("cam", "tile"), None), P(("cam", "tile"), None))
    return jax.shard_map(shards, mesh=mesh, in_specs=in_specs, out_specs=out_specs, check_vma=False)
```

```python
import math

import jax
import jax.numpy as jnp
from jax import lax
from jax.experimental import pallas as pl
from jax.experimental.pallas import tpu as pltpu
from jax.sharding import PartitionSpec as P

NX, NY, NZH, NZL, NC = 4, 4, 2, 4, 2
NZ = NZH * NZL
H = 8
HD = 32
C = H * HD
KB = 32
TQ = 128
NEG = -1e30
BIG = 3e38
SCALE = 1.0 / math.sqrt(HD)
LOG2E = math.log2(math.e)
CH = KB * NX
KEYS = 2 * NY * CH
HALF = KEYS // 2
QB = 2 * TQ
QH = QB // NC
QS = QH // NZL

F32 = jnp.float32
BF16 = jnp.bfloat16


def nt(a, b):
    return lax.dot_general(a, b, (((1,), (1,)), ((), ())), preferred_element_type=F32)


def nn(a, b):
    return jnp.dot(a, b, preferred_element_type=F32)


def remote(src, dst, send, recv, device):
    return pltpu.make_async_remote_copy(
        src_ref=src,
        dst_ref=dst,
        send_sem=send,
        recv_sem=recv,
        device_id=device,
        device_id_type=pl.DeviceIdType.MESH,
    )


def kernel(
    q_in, g_in, k_in, v_in, vis_in, cnt_in,
    gq_out, gk_out, gv_out,
    vis_i, cnt, pb, tb, in_s, kv, qd, vis, qs, gs, pbuf, dbuf, cap, kt,
    cstat, stat, stat_in, core_out, core_in, alpha, delta,
    dk, dv, rs1_out, rs1_in, rs2_own, rs2_out, rs2_in,
    dqt, dq, dq_sib, dqz_own, dqz_out, dqz_in, dqf_out, dqf_in,
    ga1_s, ga1_r, gb1_s, gb1_r, ga2_s, ga2_r, gb2_s, gb2_r,
    qx_s, qx_r, qc_s, qc_r, vx_s, vx_r,
    st_s, st_r, sc_s, sc_r,
    ra1_s, ra1_r, rb1_s, rb1_r, ra2_s, ra2_r, rb2_s, rb2_r,
    dc_s, dc_r, dz_s, dz_r, df_s, df_r,
):
    cam = lax.axis_index("cam")
    tile = lax.axis_index("tile")
    core = lax.rem(cam, NC)
    zl = lax.div(cam, NC)
    y = lax.rem(tile, NY)
    zh = lax.rem(lax.div(tile, NY), NZH)
    x = lax.div(tile, NY * NZH)
    z = zh * NZL + zl

    def at(x_, y_, z_, core_):
        zh_ = lax.div(z_, NZL)
        zl_ = lax.rem(z_, NZL)
        return {"cam": zl_ * NC + core_, "tile": (x_ * NZH + zh_) * NY + y_}

    def xp(j):
        return at(lax.rem(x + j, NX), y, z, core)

    def yp(j):
        return at(x, lax.rem(y + j, NY), z, core)

    def zp(j):
        return at(x, y, lax.rem(z + j, NZ), core)

    def fp(jz, jc):
        return at(x, y, zh * NZL + lax.rem(zl + jz, NZL), lax.rem(core + jc, NC))

    sibling = fp(0, 1)
    mirror = at(x, y, NZ - 1 - z, core)

    barrier = pltpu.get_barrier_semaphore()
    peers = [xp(j) for j in range(1, NX)] + [yp(j) for j in range(1, NY)] + [zp(j) for j in range(1, NZ)]
    peers += [fp(jz, 1) for jz in range(NZL)]
    for peer in peers:
        pl.semaphore_signal(barrier, inc=1, device_id=peer, device_id_type=pl.DeviceIdType.MESH)

    own_a = pl.multiple_of(y * CH + x * KB, KB)
    own_b = pl.multiple_of(HALF + x * CH + y * KB, KB)
    loads = [
        (k_in.at[pl.ds(0, KB)], kv.at[pl.ds(own_a, KB), pl.ds(0, C)]),
        (v_in.at[pl.ds(0, KB)], kv.at[pl.ds(own_a, KB), pl.ds(C, C)]),
        (k_in.at[pl.ds(KB, KB)], kv.at[pl.ds(own_b, KB), pl.ds(0, C)]),
        (v_in.at[pl.ds(KB, KB)], kv.at[pl.ds(own_b, KB), pl.ds(C, C)]),
        (q_in, qd.at[zh, 0]),
        (g_in, qd.at[zh, 1]),
        (vis_in, vis_i),
        (cnt_in, cnt),
    ]
    loads = [pltpu.make_async_copy(src, dst, in_s.at[n]) for n, (src, dst) in enumerate(loads)]
    for copy in loads:
        copy.start()
    for copy in loads:
        copy.wait()
    vis[zh, :2, : NX * NZH * NY * 2] = vis_i[...].astype(F32)

    pl.semaphore_wait(barrier, len(peers))

    ga1 = [remote(kv.at[pl.ds(own_a, KB)], kv.at[pl.ds(own_a, KB)], ga1_s.at[j - 1], ga1_r.at[j - 1], xp(j)) for j in range(1, NX)]
    gb1 = [remote(kv.at[pl.ds(own_b, KB)], kv.at[pl.ds(own_b, KB)], gb1_s.at[j - 1], gb1_r.at[j - 1], yp(j)) for j in range(1, NY)]
    for copy in ga1 + gb1:
        copy.start()
    qx = remote(qd.at[zh, core], qd.at[zh, core], qx_s.at[0], qx_r.at[0], mirror)
    qx.start()
    vx = remote(vis.at[zh], vis.at[zh], vx_s.at[0], vx_r.at[0], zp(NZL))
    vx.start()

    head_of = lax.broadcasted_iota(jnp.int32, (QB, C), 1) // HD

    def stack(b):
        qb = qd[b, 0]
        gb = qd[b, 1]

        def one(h, _):
            row = pl.multiple_of((b * H + h) * QB, QB)
            keep = head_of == h
            qs[pl.ds(row, QB), :] = jnp.where(keep, qb, jnp.zeros_like(qb))
            gs[pl.ds(row, QB), :] = jnp.where(keep, gb, jnp.zeros_like(gb))
            return 0

        lax.fori_loop(0, H, one, 0)

    stack(zh)

    blocks = NX * NZH * NY * 2
    row = lax.broadcasted_iota(jnp.int32, (KEYS, blocks), 0)
    col = lax.broadcasted_iota(jnp.int32, (KEYS, blocks), 1)
    half = row // HALF
    outer = (row % HALF) // CH
    inner = (row % CH) // KB
    bx = jnp.where(half == 0, inner, outer)
    by = jnp.where(half == 0, outer, inner)
    block = 2 * ((bx * NZH + zh) * NY + by) + half
    pick = ((block == col) & (row % KB < cnt[...])).astype(F32).astype(BF16)

    def cap_of(b):
        seen = jnp.concatenate(
            [jnp.broadcast_to(vis[b, t : t + 1, :blocks], (TQ, blocks)) for t in range(2)], axis=0
        ).astype(BF16)
        cap[b] = jnp.where(nt(pick, seen) > 0.5, BIG, NEG)

    cap_of(zh)

    chunk_a = pl.multiple_of(y * CH, CH)
    chunk_b = pl.multiple_of(HALF + x * CH, CH)
    for copy in ga1 + gb1:
        copy.wait_recv()
    ga2 = [remote(kv.at[pl.ds(chunk_a, CH)], kv.at[pl.ds(chunk_a, CH)], ga2_s.at[j - 1], ga2_r.at[j - 1], yp(j)) for j in range(1, NY)]
    gb2 = [remote(kv.at[pl.ds(chunk_b, CH)], kv.at[pl.ds(chunk_b, CH)], gb2_s.at[j - 1], gb2_r.at[j - 1], xp(j)) for j in range(1, NX)]
    for j in (0, 2, 1):
        ga2[j].start()
        gb2[j].start()

    def chunk_rows(i):
        ra = pl.ds(pl.multiple_of(lax.rem(y + 1 + i, NY) * CH, CH), CH)
        rb = pl.ds(pl.multiple_of(HALF + lax.rem(x + 1 + i, NX) * CH, CH), CH)
        return ra, rb

    def first(b, i):
        ra, rb = chunk_rows(i)
        kc = jnp.concatenate([kv[ra, :C], kv[rb, :C]], axis=0)
        vc = jnp.concatenate([kv[ra, C:], kv[rb, C:]], axis=0)
        n = b * NX + i
        for h in range(H):
            rows = pl.ds(pl.multiple_of((b * H + h) * QB, QB), QB)
            s = nt(kc, qs[rows, :]) * (SCALE * LOG2E)
            s = jnp.minimum(s, jnp.concatenate([cap[b, ra, :], cap[b, rb, :]], axis=0))
            m = jnp.maximum(jnp.max(s, axis=0, keepdims=True), 0.1 * NEG)
            p = jnp.exp2(s - m)
            pbuf[n, h] = p
            d = nt(vc, gs[rows, :])
            dbuf[n, h] = d
            cstat[n, 0, h : h + 1, :] = m
            cstat[n, 1, h : h + 1, :] = jnp.sum(p, axis=0, keepdims=True)
            cstat[n, 2, h : h + 1, :] = jnp.sum(p * d, axis=0, keepdims=True)

    def stat_copies(b):
        return [remote(stat.at[b], stat_in.at[b, j - 1], st_s.at[b, j - 1], st_r.at[b, j - 1], zp(j)) for j in range(1, NZ)]

    def stat_send(b):
        parts = [tuple(cstat[b * NX + i, k] for k in range(3)) for i in range(NX)]
        top = parts[0][0]
        for part in parts[1:]:
            top = jnp.maximum(top, part[0])
        total = jnp.zeros_like(top)
        dot = jnp.zeros_like(top)
        for m, l, d in parts:
            w = jnp.exp2(m - top)
            total = total + l * w
            dot = dot + d * w
        total = jnp.maximum(total, 1e-30)
        stat[b, 0] = top + jnp.log2(total)
        stat[b, 1] = dot / total
        for copy in stat_copies(b):
            copy.start()

    def core_copy(b):
        return remote(core_out.at[b], core_in.at[b], sc_s.at[b], sc_r.at[b], sibling)

    def merge(parts):
        top = parts[0][0]
        for part in parts[1:]:
            top = jnp.maximum(top, part[0])
        total = jnp.zeros_like(top)
        dot = jnp.zeros_like(top)
        for lse, mean in parts:
            w = jnp.exp2(lse - top)
            total = total + w
            dot = dot + mean * w
        return top + jnp.log2(total), dot / total

    def stat_ring(b):
        for copy in stat_copies(b):
            copy.wait_recv()
        parts = [(stat[b, 0], stat[b, 1])]
        parts += [(stat_in[b, j, 0], stat_in[b, j, 1]) for j in range(NZ - 1)]
        for k, value in enumerate(merge(parts)):
            core_out[b, k] = value
        core_copy(b).start()

    def stat_final(b):
        core_copy(b).wait_recv()
        lse, mean = merge([(core_out[b, 0], core_out[b, 1]), (core_in[b, 0], core_in[b, 1])])
        for i in range(NX):
            alpha[b * NX + i] = jnp.exp2(cstat[b * NX + i, 0] - lse)
        delta[b] = mean

    def chunk_copies(i):
        return (
            remote(rs1_out.at[i, 0], rs1_in.at[i, 0], ra1_s.at[i], ra1_r.at[i], yp(i + 1)),
            remote(rs1_out.at[i, 1], rs1_in.at[i, 1], rb1_s.at[i], rb1_r.at[i], xp(i + 1)),
        )

    def prepare(b, i, first_chunk):
        n = b * NX + i
        rows = pl.ds(pl.multiple_of(i * 2 * CH, 2 * CH), 2 * CH)
        dqs = []
        for h in range(H):
            a = alpha[n, h : h + 1, :]
            e = delta[b, h : h + 1, :]
            p = pbuf[n, h] * a
            t = (p * (dbuf[n, h] - e)).astype(BF16)
            pb[rows, h * QB : (h + 1) * QB] = p.astype(BF16)
            tb[rows, h * QB : (h + 1) * QB] = t
            dqs.append(nn(kt[i, h * HD : (h + 1) * HD, :], t))
        dqc = jnp.concatenate(dqs, axis=0)

        @pl.when(first_chunk)
        def _():
            dqt[b] = dqc

        @pl.when(jnp.logical_not(first_chunk))
        def _():
            dqt[b] = dqt[b] + dqc

    def prepare_0():
        def one(i, _):
            prepare(0, i, i == 0)
            return 0

        lax.fori_loop(0, NX, one, 0)

    def grads_0(pair):
        rows = slice(pair * 4 * CH, (pair + 1) * 4 * CH)
        dkc = nn(tb[rows, :], qs[: H * QB, :])
        dvc = nn(pb[rows, :], gs[: H * QB, :])
        for u in range(2):
            dk[2 * pair + u] = dkc[u * 2 * CH : (u + 1) * 2 * CH]
            dv[2 * pair + u] = dvc[u * 2 * CH : (u + 1) * 2 * CH]

    def second_1(lo, hi):
        def one(n, _):
            i = jnp.where(n < 2, 1 - n, n)
            rows = pl.ds(pl.multiple_of(i * 2 * CH, 2 * CH), 2 * CH)
            prepare(1, i, n == 0)
            dki = dk[i] + nn(tb[rows, :], qs[H * QB :, :])
            dvi = dv[i] + nn(pb[rows, :], gs[H * QB :, :])

            @pl.when(i < NX - 1)
            def _():
                for half in range(2):
                    rs1_out[i, half, :, :C] = dki[half * CH : (half + 1) * CH].astype(BF16)
                    rs1_out[i, half, :, C:] = dvi[half * CH : (half + 1) * CH].astype(BF16)
                for copy in chunk_copies(i):
                    copy.start()

            @pl.when(i == NX - 1)
            def _():
                dk[i] = dki
                dv[i] = dvi

            return 0

        lax.fori_loop(lo, hi, one, 0)

    other_half = pl.ds(pl.multiple_of((1 - core) * QH, QH), QH)

    def dq_core(b):
        return remote(dq.at[b, other_half], dq_sib.at[b], dc_s.at[b], dc_r.at[b], sibling)

    def dq_start(b):
        dq[b] = dqt[b].T * SCALE
        dq_core(b).start()

    def dq_slot(b, j):
        return remote(
            dqz_out.at[b, pl.ds(j * QS, QS)],
            dqz_in.at[z],
            dz_s.at[b * NZL + j],
            dz_r.at[z],
            at(x, y, b * NZL + j, core),
        )

    def dq_ring(b):
        dq_core(b).wait_recv()
        mine = dq[b, pl.ds(pl.multiple_of(core * QH, QH), QH), :] + dq_sib[b]
        dqz_out[b] = mine.astype(BF16)
        for j in range(NZL):

            @pl.when(z == b * NZL + j)
            def _(j=j):
                dqz_own[...] = mine[j * QS : (j + 1) * QS, :]

            @pl.when(z != b * NZL + j)
            def _(j=j):
                dq_slot(b, j).start()

    first(zh, NX - 1)
    vx.wait_recv()
    cap_of(1 - zh)
    qx.wait_recv()
    qc = remote(qd.at[1 - zh, core], qd.at[1 - zh, core], qc_s.at[0], qc_r.at[0], sibling)
    qc.start()
    qc.wait_recv()
    stack(1 - zh)

    def unit(n, _):
        for step, j in enumerate((2, 0, 1)):

            @pl.when(n == step)
            def _(j=j):
                ga2[j].wait_recv()
                gb2[j].wait_recv()

        in_0 = NX - 1 + zh
        b = (n >= in_0).astype(jnp.int32)
        place = jnp.where(b == 0, n + 1 - zh, n - in_0 + zh)
        i = jnp.where(place == 0, NX - 1, jnp.where(place == 1, 0, jnp.where(place == 2, 2, 1)))
        first(b, i)

        @pl.when(n == in_0 - 1)
        def _():
            stat_send(0)

        return 0

    lax.fori_loop(0, NZH * NX - 1, unit, 0)
    stat_send(1)
    for i in range(NX):
        ra, rb = chunk_rows(i)
        kt[i] = jnp.concatenate([kv[ra, :C], kv[rb, :C]], axis=0).astype(F32).T.astype(BF16)
    stat_ring(0)
    stat_final(0)
    prepare_0()
    dq_start(0)
    grads_0(0)
    stat_ring(1)
    grads_0(1)
    stat_final(1)
    second_1(0, 2)
    dq_ring(0)
    second_1(2, NX)
    dq_start(1)

    dq_ring(1)
    for i in range(NX - 1):
        for copy in chunk_copies(i):
            copy.wait_recv()
    for half in range(2):
        for part, acc in enumerate((dk, dv)):
            cols = slice(part * C, (part + 1) * C)
            total = acc[NX - 1, half * CH : (half + 1) * CH, :]
            for i in range(NX - 1):
                total = total + rs1_in[i, half, :, cols].astype(F32)
            rs2_own[half, :, cols] = total
            rs2_out[half, :, cols] = total.astype(BF16)

    def rs2_copies(j):
        rows_a = pl.ds(pl.multiple_of(lax.rem(x + j, NX) * KB, KB), KB)
        rows_b = pl.ds(pl.multiple_of(lax.rem(y + j, NY) * KB, KB), KB)
        return (
            remote(rs2_out.at[0, rows_a], rs2_in.at[j - 1, 0], ra2_s.at[j - 1], ra2_r.at[j - 1], xp(j)),
            remote(rs2_out.at[1, rows_b], rs2_in.at[j - 1, 1], rb2_s.at[j - 1], rb2_r.at[j - 1], yp(j)),
        )

    for j in range(1, NX):
        for copy in rs2_copies(j):
            copy.start()

    total = dqz_own[...]
    for j in range(1, NZ):
        sender = lax.rem(z + j, NZ)
        remote(dqz_out.at[0, pl.ds(0, QS)], dqz_in.at[sender], dz_s.at[0], dz_r.at[sender], sibling).wait_recv()
        total = total + dqz_in[sender].astype(F32)
    dqf_out[...] = total.astype(BF16)

    def dqf_copy(jz, jc):
        k = jz * NC + jc - 1
        return remote(dqf_out, dqf_in.at[k], df_s.at[k], df_r.at[k], fp(jz, jc))

    others = [(jz, jc) for jz in range(NZL) for jc in range(NC) if jz + jc > 0]
    for jz, jc in others:
        dqf_copy(jz, jc).start()
    gq_out[pl.ds(pl.multiple_of(core * QH + zl * QS, QS), QS), :] = dqf_out[...]

    for j in range(1, NX):
        for copy in rs2_copies(j):
            copy.wait_recv()
    for half, pos in ((0, x), (1, y)):
        rows = pl.ds(pl.multiple_of(pos * KB, KB), KB)
        total = rs2_own[half, rows, :]
        for j in range(NX - 1):
            total = total + rs2_in[j, half].astype(F32)
        gk_out[half * KB : (half + 1) * KB, :] = (total[:, :C] * SCALE).astype(BF16)
        gv_out[half * KB : (half + 1) * KB, :] = total[:, C:].astype(BF16)

    for jz, jc in others:
        dqf_copy(jz, jc).wait_recv()
        fz = lax.rem(zl - jz + NZL, NZL)
        fc = lax.rem(core - jc + NC, NC)
        gq_out[pl.ds(pl.multiple_of(fc * QH + fz * QS, QS), QS), :] = dqf_in[jz * NC + jc - 1]

    for copy in ga1 + gb1 + ga2 + gb2 + [qx, vx, qc]:
        copy.wait_send()
    for b in range(NZH):
        for copy in stat_copies(b):
            copy.wait_send()
        core_copy(b).wait_send()
        dq_core(b).wait_send()
        for j in range(NZL):

            @pl.when(z != b * NZL + j)
            def _(b=b, j=j):
                dq_slot(b, j).wait_send()

    for i in range(NX - 1):
        for copy in chunk_copies(i):
            copy.wait_send()
    for j in range(1, NX):
        for copy in rs2_copies(j):
            copy.wait_send()
    for jz, jc in others:
        dqf_copy(jz, jc).wait_send()


def write_out(a, b, c, a_out, b_out, c_out, sem):
    copies = [
        pltpu.make_async_copy(src, dst, sem.at[n])
        for n, (src, dst) in enumerate(((a, a_out), (b, b_out), (c, c_out)))
    ]
    for copy in copies:
        copy.start()
    for copy in copies:
        copy.wait()


def shards(queries, keys, values, grad_out, visible, counts):
    vmem = pl.BlockSpec(memory_space=pltpu.VMEM)
    dma = pltpu.SemaphoreType.DMA
    V = pltpu.VMEM
    blocks = NX * NZH * NY * 2
    scratch = [
        V((2, blocks), jnp.int32),
        V((1, blocks), jnp.int32),
        V((KEYS, H * QB), BF16),
        V((KEYS, H * QB), BF16),
        dma((8,)),
        V((KEYS, 2 * C), BF16),
        V((NZH, 2, QB, C), BF16),
        V((NZH, 8, 128), F32),
        V((NZH * H * QB, C), BF16),
        V((NZH * H * QB, C), BF16),
        V((NZH * NX, H, 2 * CH, QB), F32),
        V((NZH * NX, H, 2 * CH, QB), F32),
        V((NZH, KEYS, QB), F32),
        V((NX, C, 2 * CH), BF16),
        V((NZH * NX, 3, H, QB), F32),
        V((NZH, 2, H, QB), F32),
        V((NZH, NZ - 1, 2, H, QB), F32),
        V((NZH, 2, H, QB), F32),
        V((NZH, 2, H, QB), F32),
        V((NZH * NX, H, QB), F32),
        V((NZH, H, QB), F32),
        V((NX, 2 * CH, C), F32),
        V((NX, 2 * CH, C), F32),
        V((NX - 1, 2, CH, 2 * C), BF16),
        V((NX - 1, 2, CH, 2 * C), BF16),
        V((2, CH, 2 * C), F32),
        V((2, CH, 2 * C), BF16),
        V((NX - 1, 2, KB, 2 * C), BF16),
        V((NZH, C, QB), F32),
        V((NZH, QB, C), F32),
        V((NZH, QH, C), F32),
        V((QS, C), F32),
        V((NZH, QH, C), BF16),
        V((NZ, QS, C), BF16),
        V((QS, C), BF16),
        V((NZL * NC - 1, QS, C), BF16),
    ]
    sems = [(NX - 1,)] * 8 + [(1,)] * 6 + [(NZH, NZ - 1)] * 2 + [(NZH,)] * 2 + [(NX - 1,)] * 8
    sems += [(NZH,)] * 2 + [(NZ,)] * 2 + [(NZL * NC - 1,)] * 2
    scratch += [dma(s) for s in sems]
    shapes = [(QB, C), (2 * KB, C), (2 * KB, C)]
    anywhere = pl.BlockSpec(memory_space=pl.ANY)
    grads = pl.pallas_call(
        kernel,
        out_shape=tuple(pltpu.VMEM(s, BF16) for s in shapes),
        in_specs=[anywhere] * 6,
        out_specs=(vmem,) * 3,
        scratch_shapes=scratch,
        compiler_params=pltpu.CompilerParams(
            collective_id=0, has_side_effects=True, vmem_limit_bytes=62 * 1024 * 1024
        ),
    )(queries, grad_out, keys, values, visible, counts.reshape(1, -1))
    grads = [pltpu.with_memory_space_constraint(g, pltpu.VMEM) for g in grads]
    return pl.pallas_call(
        write_out,
        out_shape=tuple(jax.ShapeDtypeStruct(s, BF16) for s in shapes),
        in_specs=[vmem] * 3,
        out_specs=(anywhere,) * 3,
        scratch_shapes=[dma((3,))],
    )(*grads)


def solution(mesh):
    in_specs = (
        P("tile", None),
        P(("cam", "tile"), None),
        P(("cam", "tile"), None),
        P("tile", None),
        P("tile", "cam"),
        P("cam"),
    )
    out_specs = (P("tile", None), P(("cam", "tile"), None), P(("cam", "tile"), None))
    return jax.shard_map(shards, mesh=mesh, in_specs=in_specs, out_specs=out_specs, check_vma=False)
```

```python
import math

import jax
import jax.numpy as jnp
from jax import lax
from jax.experimental import pallas as pl
from jax.experimental.pallas import tpu as pltpu
from jax.sharding import PartitionSpec as P

NX, NY, NZH, NZL, NC = 4, 4, 2, 4, 2
NZ = NZH * NZL
H = 8
HD = 32
C = H * HD
KB = 32
TQ = 128
NEG = -1e30
BIG = 3e38
SCALE = 1.0 / math.sqrt(HD)
LOG2E = math.log2(math.e)
CH = KB * NX
KEYS = 2 * NY * CH
HALF = KEYS // 2
QB = 2 * TQ
QH = QB // NC
QS = QH // NZL

F32 = jnp.float32
BF16 = jnp.bfloat16


def nt(a, b):
    return lax.dot_general(a, b, (((1,), (1,)), ((), ())), preferred_element_type=F32)


def nn(a, b):
    return jnp.dot(a, b, preferred_element_type=F32)


def remote(src, dst, send, recv, device):
    return pltpu.make_async_remote_copy(
        src_ref=src,
        dst_ref=dst,
        send_sem=send,
        recv_sem=recv,
        device_id=device,
        device_id_type=pl.DeviceIdType.MESH,
    )


def kernel(
    q_in, g_in, k_in, v_in, vis_in, cnt_in,
    gq_out, gk_out, gv_out,
    vis_i, cnt, pb, tb, in_s, kv, qd, vis, qs, gs, pbuf, dbuf, cap, kt,
    cstat, stat, stat_in, core_out, core_in, alpha, delta,
    dk, dv, rs1_out, rs1_in, rs2_own, rs2_out, rs2_in,
    dqt, dq, dq_sib, dqz_own, dqz_out, dqz_in, dqf_out, dqf_in,
    ga0_s, ga0_r, gb0_s, gb0_r, ga1_s, ga1_r, gb1_s, gb1_r, ga2_s, ga2_r, gb2_s, gb2_r,
    qx_s, qx_r, qc_s, qc_r, vx_s, vx_r,
    st_s, st_r, sc_s, sc_r,
    ra1_s, ra1_r, rb1_s, rb1_r, ra2_s, ra2_r, rb2_s, rb2_r,
    dc_s, dc_r, dz_s, dz_r, df_s, df_r,
):
    cam = lax.axis_index("cam")
    tile = lax.axis_index("tile")
    core = lax.rem(cam, NC)
    zl = lax.div(cam, NC)
    y = lax.rem(tile, NY)
    zh = lax.rem(lax.div(tile, NY), NZH)
    x = lax.div(tile, NY * NZH)
    z = zh * NZL + zl

    def at(x_, y_, z_, core_):
        zh_ = lax.div(z_, NZL)
        zl_ = lax.rem(z_, NZL)
        return {"cam": zl_ * NC + core_, "tile": (x_ * NZH + zh_) * NY + y_}

    def xp(j):
        return at(lax.rem(x + j, NX), y, z, core)

    def yp(j):
        return at(x, lax.rem(y + j, NY), z, core)

    def zp(j):
        return at(x, y, lax.rem(z + j, NZ), core)

    def fp(jz, jc):
        return at(x, y, zh * NZL + lax.rem(zl + jz, NZL), lax.rem(core + jc, NC))

    sibling = fp(0, 1)
    mirror = at(x, y, NZ - 1 - z, core)

    barrier = pltpu.get_barrier_semaphore()
    peers = [xp(j) for j in range(1, NX)] + [yp(j) for j in range(1, NY)] + [zp(j) for j in range(1, NZ)]
    peers += [fp(jz, 1) for jz in range(NZL)]
    for peer in peers:
        pl.semaphore_signal(barrier, inc=1, device_id=peer, device_id_type=pl.DeviceIdType.MESH)

    LANES = C // 2
    loads = [
        (k_in.at[pl.ds(0, KB)], kv.at[pl.ds(0, KB), pl.ds(0, C)]),
        (v_in.at[pl.ds(0, KB)], kv.at[pl.ds(0, KB), pl.ds(C, C)]),
        (k_in.at[pl.ds(KB, KB)], kv.at[pl.ds(CH, KB), pl.ds(0, C)]),
        (v_in.at[pl.ds(KB, KB)], kv.at[pl.ds(CH, KB), pl.ds(C, C)]),
        (vis_in, vis_i),
        (cnt_in, cnt),
    ]
    for part in range(2):
        lanes = pl.ds(part * LANES, LANES)
        loads += [(q_in.at[:, lanes], qd.at[zh, part, 0]), (g_in.at[:, lanes], qd.at[zh, part, 1])]
    loads = [pltpu.make_async_copy(src, dst, in_s.at[n]) for n, (src, dst) in enumerate(loads)]
    for copy in loads:
        copy.start()
    for copy in loads:
        copy.wait()
    vis[zh, :2, : NX * NZH * NY * 2] = vis_i[...].astype(F32)

    pl.semaphore_wait(barrier, len(peers))

    def rows_to(src, dst, count, sems, j, device):
        return remote(kv.at[pl.ds(src, count)], kv.at[pl.ds(dst, count)], sems[0].at[j - 1], sems[1].at[j - 1], device)

    js = range(1, NX)
    ga1 = [rows_to(0, (NX - j) * KB, KB, (ga1_s, ga1_r), j, xp(j)) for j in js]
    gb1 = [rows_to(CH, CH + (NY - j) * KB, KB, (gb1_s, gb1_r), j, yp(j)) for j in js]
    place = {0: 0, 1: 1, NX - 1: 2, 2: 3}
    ga0 = [rows_to(0, place[NY - j] * 2 * CH, KB, (ga0_s, ga0_r), j, yp(j)) for j in js]
    gb0 = [rows_to(CH, place[NX - j] * 2 * CH + CH, KB, (gb0_s, gb0_r), j, xp(j)) for j in js]
    ga2 = [rows_to(KB, place[NY - j] * 2 * CH + KB, CH - KB, (ga2_s, ga2_r), j, yp(j)) for j in js]
    gb2 = [rows_to(CH + KB, place[NX - j] * 2 * CH + CH + KB, CH - KB, (gb2_s, gb2_r), j, xp(j)) for j in js]
    qx = [remote(qd.at[zh, part, core], qd.at[zh, part, core], qx_s.at[part], qx_r.at[part], mirror) for part in range(2)]
    qc = [remote(qd.at[1 - zh, part, core], qd.at[1 - zh, part, core], qc_s.at[part], qc_r.at[part], sibling) for part in range(2)]
    for copy in ga1 + gb1:
        copy.start()
    qx[0].start()
    qx[1].start()
    vx = remote(vis.at[zh], vis.at[zh], vx_s.at[0], vx_r.at[0], zp(NZL))
    vx.start()
    for copy in ga0 + gb0:
        copy.start()

    head_of = lax.broadcasted_iota(jnp.int32, (QB, LANES), 1) // HD

    def stack(b, part):
        qb = qd[b, part, 0]
        gb = qd[b, part, 1]
        zero = jnp.zeros_like(qb)

        def one(h, _):
            rows = pl.ds(pl.multiple_of((b * H + part * (H // 2) + h) * QB, QB), QB)
            keep = head_of == h
            for ref, block in ((qs, qb), (gs, gb)):
                ref[rows, part * LANES : (part + 1) * LANES] = jnp.where(keep, block, zero)
                ref[rows, (1 - part) * LANES : (2 - part) * LANES] = zero
            return 0

        lax.fori_loop(0, H // 2, one, 0)

    stack(zh, 0)
    stack(zh, 1)

    blocks = NX * NZH * NY * 2
    row = lax.broadcasted_iota(jnp.int32, (KEYS, blocks), 0)
    col = lax.broadcasted_iota(jnp.int32, (KEYS, blocks), 1)
    half = (row % (2 * CH)) // CH
    outer = row // (2 * CH)
    outer = jnp.where(outer == 3, 2, jnp.where(outer == 2, 3, outer))
    inner = (row % CH) // KB
    bx = (x + jnp.where(half == 0, inner, outer)) % NX
    by = (y + jnp.where(half == 0, outer, inner)) % NY
    block = 2 * ((bx * NZH + zh) * NY + by) + half
    pick = ((block == col) & (row % KB < cnt[...])).astype(F32).astype(BF16)

    def cap_of(b):
        seen = jnp.concatenate(
            [jnp.broadcast_to(vis[b, t : t + 1, :blocks], (TQ, blocks)) for t in range(2)], axis=0
        ).astype(BF16)
        cap[b] = jnp.where(nt(pick, seen) > 0.5, BIG, NEG)

    cap_of(zh)

    for one_stage, next_stage in ((ga1, ga2), (gb1, gb2)):
        for copy in one_stage:
            copy.wait_recv()
        for j in (0, 2, 1):
            next_stage[j].start()

    def chunk_rows(i, count=1):
        return pl.ds(i * 2 * CH, count * 2 * CH)

    def first(b, i, count, heads):
        rk = chunk_rows(i, count)
        kc = kv[rk, :C]
        vc = kv[rk, C:]
        for h in heads:
            rows = pl.ds(pl.multiple_of((b * H + h) * QB, QB), QB)
            s = nt(kc, qs[rows, :]) * (SCALE * LOG2E)
            s = jnp.minimum(s, cap[b, rk, :])
            m = jnp.maximum(jnp.max(s, axis=0, keepdims=True), 0.1 * NEG)
            p = jnp.exp2(s - m)
            d = nt(vc, gs[rows, :])
            for u in range(count):
                pbuf[b * NX + i + u, h] = p[u * 2 * CH : (u + 1) * 2 * CH]
                dbuf[b * NX + i + u, h] = d[u * 2 * CH : (u + 1) * 2 * CH]
            group = b * 3 + min(i, 1) + (i == 3)
            cstat[group, 0, h : h + 1, :] = m
            cstat[group, 1, h : h + 1, :] = jnp.sum(p, axis=0, keepdims=True)
            cstat[group, 2, h : h + 1, :] = jnp.sum(p * d, axis=0, keepdims=True)

    def stat_copies(b):
        return [remote(stat.at[b], stat_in.at[b, j - 1], st_s.at[b, j - 1], st_r.at[b, j - 1], zp(j)) for j in range(1, NZ)]

    def stat_send(b):
        parts = [tuple(cstat[b * 3 + i, k] for k in range(3)) for i in range(3)]
        top = parts[0][0]
        for part in parts[1:]:
            top = jnp.maximum(top, part[0])
        total = jnp.zeros_like(top)
        dot = jnp.zeros_like(top)
        for m, l, d in parts:
            w = jnp.exp2(m - top)
            total = total + l * w
            dot = dot + d * w
        total = jnp.maximum(total, 1e-30)
        stat[b, 0] = top + jnp.log2(total)
        stat[b, 1] = dot / total
        copies = stat_copies(b)
        for j in (4, 3, 5, 2, 6, 1, 7):
            copies[j - 1].start()

    def core_copy(b):
        return remote(core_out.at[b], core_in.at[b], sc_s.at[b], sc_r.at[b], sibling)

    def merge(parts):
        top = parts[0][0]
        for part in parts[1:]:
            top = jnp.maximum(top, part[0])
        total = jnp.zeros_like(top)
        dot = jnp.zeros_like(top)
        for lse, mean in parts:
            w = jnp.exp2(lse - top)
            total = total + w
            dot = dot + mean * w
        return top + jnp.log2(total), dot / total

    def stat_ring(b):
        for copy in stat_copies(b):
            copy.wait_recv()
        parts = [(stat[b, 0], stat[b, 1])]
        parts += [(stat_in[b, j, 0], stat_in[b, j, 1]) for j in range(NZ - 1)]
        for k, value in enumerate(merge(parts)):
            core_out[b, k] = value
        core_copy(b).start()

    def stat_final(b):
        core_copy(b).wait_recv()
        lse, mean = merge([(core_out[b, 0], core_out[b, 1]), (core_in[b, 0], core_in[b, 1])])
        for i in range(3):
            alpha[b * 3 + i] = jnp.exp2(cstat[b * 3 + i, 0] - lse)
        delta[b] = mean

    def chunk_copies(i):
        r = jnp.where(i == 3, 2, jnp.where(i == 2, 3, 1))
        return (
            remote(rs1_out.at[i - 1, 0], rs1_in.at[r - 1, 0], ra1_s.at[r - 1], ra1_r.at[r - 1], yp(r)),
            remote(rs1_out.at[i - 1, 1], rs1_in.at[r - 1, 1], rb1_s.at[r - 1], rb1_r.at[r - 1], xp(r)),
        )

    def prepare(b, i, first_chunk):
        n = b * NX + i
        group = b * 3 + jnp.where(i == 0, 0, jnp.where(i == 3, 2, 1))
        rows = pl.ds(pl.multiple_of(i * 2 * CH, 2 * CH), 2 * CH)
        dqs = []
        for h in range(H):
            a = alpha[group, h : h + 1, :]
            e = delta[b, h : h + 1, :]
            p = pbuf[n, h] * a
            t = (p * (dbuf[n, h] - e)).astype(BF16)
            pb[rows, h * QB : (h + 1) * QB] = p.astype(BF16)
            tb[rows, h * QB : (h + 1) * QB] = t
            dqs.append(nn(kt[i, h * HD : (h + 1) * HD, :], t))
        dqc = jnp.concatenate(dqs, axis=0)

        @pl.when(first_chunk)
        def _():
            dqt[b] = dqc

        @pl.when(jnp.logical_not(first_chunk))
        def _():
            dqt[b] = dqt[b] + dqc

    def prepare_0():
        def one(i, _):
            prepare(0, i, i == 0)
            return 0

        lax.fori_loop(0, NX, one, 0)

    def grads_0(pair):
        rows = slice(pair * 4 * CH, (pair + 1) * 4 * CH)
        dkc = nn(tb[rows, :], qs[: H * QB, :])
        dvc = nn(pb[rows, :], gs[: H * QB, :])
        for u in range(2):
            dk[2 * pair + u] = dkc[u * 2 * CH : (u + 1) * 2 * CH]
            dv[2 * pair + u] = dvc[u * 2 * CH : (u + 1) * 2 * CH]

    def second_1(lo, hi):
        def one(n, _):
            i = jnp.where(n == 0, 3, jnp.where(n == 3, 0, n))
            rows = pl.ds(pl.multiple_of(i * 2 * CH, 2 * CH), 2 * CH)
            prepare(1, i, n == 0)
            dki = dk[i] + nn(tb[rows, :], qs[H * QB :, :])
            dvi = dv[i] + nn(pb[rows, :], gs[H * QB :, :])

            @pl.when(i > 0)
            def _():
                for half in range(2):
                    rs1_out[i - 1, half, :, :C] = dki[half * CH : (half + 1) * CH].astype(BF16)
                    rs1_out[i - 1, half, :, C:] = dvi[half * CH : (half + 1) * CH].astype(BF16)
                for copy in chunk_copies(i):
                    copy.start()

            @pl.when(i == 0)
            def _():
                dk[i] = dki
                dv[i] = dvi

            return 0

        lax.fori_loop(lo, hi, one, 0)

    other_half = pl.ds(pl.multiple_of((1 - core) * QH, QH), QH)

    def dq_core(b):
        return remote(dq.at[b, other_half], dq_sib.at[b], dc_s.at[b], dc_r.at[b], sibling)

    def dq_start(b):
        dq[b] = dqt[b].T * SCALE
        dq_core(b).start()

    def dq_slot(b, j):
        return remote(
            dqz_out.at[b, pl.ds(j * QS, QS)],
            dqz_in.at[z],
            dz_s.at[b * NZL + j],
            dz_r.at[z],
            at(x, y, b * NZL + j, core),
        )

    def dq_ring(b):
        dq_core(b).wait_recv()
        mine = dq[b, pl.ds(pl.multiple_of(core * QH, QH), QH), :] + dq_sib[b]
        dqz_out[b] = mine.astype(BF16)
        for j in range(NZL):

            @pl.when(z == b * NZL + j)
            def _(j=j):
                dqz_own[...] = mine[j * QS : (j + 1) * QS, :]

            @pl.when(z != b * NZL + j)
            def _(j=j):
                dq_slot(b, j).start()

    head_parts = (range(H // 2), range(H // 2, H))
    first(zh, 0, 1, range(H))
    vx.wait_recv()
    cap_of(1 - zh)
    for part, heads in enumerate(head_parts):
        qx[part].wait_recv()
        qc[part].start()
        qc[part].wait_recv()
        stack(1 - zh, part)
        first(1 - zh, 0, 1, heads)

    def shard(b, _):
        @pl.when(b == 0)
        def _():
            for j in (0, 2):
                for copies in (ga0, gb0, ga2, gb2):
                    copies[j].wait_recv()

        first(b, 1, 2, range(H))

        @pl.when(b == 0)
        def _():
            for copies in (ga0, gb0, ga2, gb2):
                copies[1].wait_recv()

        first(b, 3, 1, range(H))
        stat_send(b)
        return 0

    lax.fori_loop(0, NZH, shard, 0)
    for i in range(NX):
        kt[i] = kv[i * 2 * CH : (i + 1) * 2 * CH, :C].astype(F32).T.astype(BF16)
    for copy in ga0 + gb0 + ga1 + gb1 + ga2 + gb2 + qx + qc + [vx]:
        copy.wait_send()
    stat_ring(0)
    stat_final(0)
    prepare_0()
    dq_start(0)
    grads_0(0)
    stat_ring(1)
    grads_0(1)
    stat_final(1)
    second_1(0, 2)
    dq_ring(0)
    second_1(2, NX)
    dq_start(1)

    dq_ring(1)
    def rs2_copies(j):
        rows = pl.ds(j * KB, KB)
        return (
            remote(rs2_out.at[0, rows], rs2_in.at[j - 1, 0], ra2_s.at[j - 1], ra2_r.at[j - 1], xp(j)),
            remote(rs2_out.at[1, rows], rs2_in.at[j - 1, 1], rb2_s.at[j - 1], rb2_r.at[j - 1], yp(j)),
        )

    for half in range(2):
        for r in js:
            chunk_copies(r)[half].wait_recv()
        for part, acc in enumerate((dk, dv)):
            cols = slice(part * C, (part + 1) * C)
            total = acc[0, half * CH : (half + 1) * CH, :]
            for i in range(NX - 1):
                total = total + rs1_in[i, half, :, cols].astype(F32)
            rs2_own[half, :, cols] = total[:KB]
            rs2_out[half, :, cols] = total.astype(BF16)
        for j in (2, 1, 3):
            rs2_copies(j)[half].start()

    total = dqz_own[...]
    for j in range(1, NZ):
        sender = lax.rem(z + j, NZ)
        remote(dqz_out.at[0, pl.ds(0, QS)], dqz_in.at[sender], dz_s.at[0], dz_r.at[sender], sibling).wait_recv()
        total = total + dqz_in[sender].astype(F32)
    dqf_out[...] = total.astype(BF16)

    def dqf_copy(jz, jc):
        k = jz * NC + jc - 1
        return remote(dqf_out, dqf_in.at[k], df_s.at[k], df_r.at[k], fp(jz, jc))

    others = [(jz, jc) for jz in range(NZL) for jc in range(NC) if jz + jc > 0]
    for jz, jc in others:
        dqf_copy(jz, jc).start()
    gq_out[pl.ds(pl.multiple_of(core * QH + zl * QS, QS), QS), :] = dqf_out[...]

    for b in range(NZH):
        for copy in stat_copies(b):
            copy.wait_send()
        core_copy(b).wait_send()
        dq_core(b).wait_send()
        for j in range(NZL):

            @pl.when(z != b * NZL + j)
            def _(b=b, j=j):
                dq_slot(b, j).wait_send()

    for r in js:
        for copy in chunk_copies(r):
            copy.wait_send()
    for j in range(1, NX):
        for copy in rs2_copies(j):
            copy.wait_recv()
    for half in range(2):
        total = rs2_own[half]
        for j in range(NX - 1):
            total = total + rs2_in[j, half].astype(F32)
        gk_out[half * KB : (half + 1) * KB, :] = (total[:, :C] * SCALE).astype(BF16)
        gv_out[half * KB : (half + 1) * KB, :] = total[:, C:].astype(BF16)

    for jz, jc in others:
        dqf_copy(jz, jc).wait_recv()
        fz = lax.rem(zl - jz + NZL, NZL)
        fc = lax.rem(core - jc + NC, NC)
        gq_out[pl.ds(pl.multiple_of(fc * QH + fz * QS, QS), QS), :] = dqf_in[jz * NC + jc - 1]

    for j in js:
        for copy in rs2_copies(j):
            copy.wait_send()
    for jz, jc in others:
        dqf_copy(jz, jc).wait_send()


def write_out(a, b, c, a_out, b_out, c_out, sem):
    copies = [
        pltpu.make_async_copy(src, dst, sem.at[n])
        for n, (src, dst) in enumerate(((a, a_out), (b, b_out), (c, c_out)))
    ]
    for copy in copies:
        copy.start()
    for copy in copies:
        copy.wait()


def shards(queries, keys, values, grad_out, visible, counts):
    vmem = pl.BlockSpec(memory_space=pltpu.VMEM)
    dma = pltpu.SemaphoreType.DMA
    V = pltpu.VMEM
    blocks = NX * NZH * NY * 2
    scratch = [
        V((2, blocks), jnp.int32),
        V((1, blocks), jnp.int32),
        V((KEYS, H * QB), BF16),
        V((KEYS, H * QB), BF16),
        dma((10,)),
        V((KEYS, 2 * C), BF16),
        V((NZH, 2, 2, QB, C // 2), BF16),
        V((NZH, 8, 128), F32),
        V((NZH * H * QB, C), BF16),
        V((NZH * H * QB, C), BF16),
        V((NZH * NX, H, 2 * CH, QB), F32),
        V((NZH * NX, H, 2 * CH, QB), F32),
        V((NZH, KEYS, QB), F32),
        V((NX, C, 2 * CH), BF16),
        V((NZH * 3, 3, H, QB), F32),
        V((NZH, 2, H, QB), F32),
        V((NZH, NZ - 1, 2, H, QB), F32),
        V((NZH, 2, H, QB), F32),
        V((NZH, 2, H, QB), F32),
        V((NZH * 3, H, QB), F32),
        V((NZH, H, QB), F32),
        V((NX, 2 * CH, C), F32),
        V((NX, 2 * CH, C), F32),
        V((NX - 1, 2, CH, 2 * C), BF16),
        V((NX - 1, 2, CH, 2 * C), BF16),
        V((2, KB, 2 * C), F32),
        V((2, CH, 2 * C), BF16),
        V((NX - 1, 2, KB, 2 * C), BF16),
        V((NZH, C, QB), F32),
        V((NZH, QB, C), F32),
        V((NZH, QH, C), F32),
        V((QS, C), F32),
        V((NZH, QH, C), BF16),
        V((NZ, QS, C), BF16),
        V((QS, C), BF16),
        V((NZL * NC - 1, QS, C), BF16),
    ]
    sems = [(NX - 1,)] * 12 + [(2,)] * 6 + [(NZH, NZ - 1)] * 2 + [(NZH,)] * 2 + [(NX - 1,)] * 8
    sems += [(NZH,)] * 2 + [(NZ,)] * 2 + [(NZL * NC - 1,)] * 2
    scratch += [dma(s) for s in sems]
    shapes = [(QB, C), (2 * KB, C), (2 * KB, C)]
    anywhere = pl.BlockSpec(memory_space=pl.ANY)
    grads = pl.pallas_call(
        kernel,
        out_shape=tuple(pltpu.VMEM(s, BF16) for s in shapes),
        in_specs=[anywhere] * 6,
        out_specs=(vmem,) * 3,
        scratch_shapes=scratch,
        compiler_params=pltpu.CompilerParams(
            collective_id=0, has_side_effects=True, vmem_limit_bytes=62 * 1024 * 1024
        ),
    )(queries, grad_out, keys, values, visible, counts.reshape(1, -1))
    grads = [pltpu.with_memory_space_constraint(g, pltpu.VMEM) for g in grads]
    return pl.pallas_call(
        write_out,
        out_shape=tuple(jax.ShapeDtypeStruct(s, BF16) for s in shapes),
        in_specs=[vmem] * 3,
        out_specs=(anywhere,) * 3,
        scratch_shapes=[dma((3,))],
    )(*grads)


def solution(mesh):
    in_specs = (
        P("tile", None),
        P(("cam", "tile"), None),
        P(("cam", "tile"), None),
        P("tile", None),
        P("tile", "cam"),
        P("cam"),
    )
    out_specs = (P("tile", None), P(("cam", "tile"), None), P(("cam", "tile"), None))
    return jax.shard_map(shards, mesh=mesh, in_specs=in_specs, out_specs=out_specs, check_vma=False)
```

```python
import math

import jax
import jax.numpy as jnp
from jax import lax
from jax.experimental import pallas as pl
from jax.experimental.pallas import tpu as pltpu
from jax.sharding import PartitionSpec as P

NX, NY, NZH, NZL, NC = 4, 4, 2, 4, 2
NZ = NZH * NZL
H = 8
HD = 32
C = H * HD
KB = 32
TQ = 128
NEG = -1e30
BIG = 3e38
SCALE = 1.0 / math.sqrt(HD)
LOG2E = math.log2(math.e)
CH = KB * NX
KEYS = 2 * NY * CH
HALF = KEYS // 2
QB = 2 * TQ
QH = QB // NC
QS = QH // NZL

F32 = jnp.float32
BF16 = jnp.bfloat16


def nt(a, b):
    return lax.dot_general(a, b, (((1,), (1,)), ((), ())), preferred_element_type=F32)


def nn(a, b):
    return jnp.dot(a, b, preferred_element_type=F32)


def remote(src, dst, send, recv, device):
    return pltpu.make_async_remote_copy(
        src_ref=src,
        dst_ref=dst,
        send_sem=send,
        recv_sem=recv,
        device_id=device,
        device_id_type=pl.DeviceIdType.MESH,
    )


def kernel(
    q_in, g_in, k_in, v_in, vis_in, cnt_in,
    gq_out, gk_out, gv_out,
    vis_i, cnt, pb_0, pb_1, tb_0, tb_1, in_s, kv, qd, vis, qs, gs, pbuf, dbuf, cap, kt,
    cstat, stat, stat_in, core_out, core_in, alpha, delta,
    dk, dv, rs1_out, rs1_in, rs2_own, rs2_out, rs2_in,
    dqt, dq, dq_sib, dqz_own, dqz_out, dqz_in, dqf_out, dqf_in,
    ga0_s, ga0_r, gb0_s, gb0_r, ga1_s, ga1_r, gb1_s, gb1_r, ga2_s, ga2_r, gb2_s, gb2_r,
    qx_s, qx_r, qc_s, qc_r, vx_s, vx_r,
    st_s, st_r, sc_s, sc_r,
    ra1_s, ra1_r, rb1_s, rb1_r, ra2_s, ra2_r, rb2_s, rb2_r,
    dc_s, dc_r, dz_s, dz_r, df_s, df_r,
):
    pb = (pb_0, pb_1)
    tb = (tb_0, tb_1)
    cam = lax.axis_index("cam")
    tile = lax.axis_index("tile")
    core = lax.rem(cam, NC)
    zl = lax.div(cam, NC)
    y = lax.rem(tile, NY)
    zh = lax.rem(lax.div(tile, NY), NZH)
    x = lax.div(tile, NY * NZH)
    z = zh * NZL + zl

    def at(x_, y_, z_, core_):
        zh_ = lax.div(z_, NZL)
        zl_ = lax.rem(z_, NZL)
        return {"cam": zl_ * NC + core_, "tile": (x_ * NZH + zh_) * NY + y_}

    def xp(j):
        return at(lax.rem(x + j, NX), y, z, core)

    def yp(j):
        return at(x, lax.rem(y + j, NY), z, core)

    def zp(j):
        return at(x, y, lax.rem(z + j, NZ), core)

    def fp(jz, jc):
        return at(x, y, zh * NZL + lax.rem(zl + jz, NZL), lax.rem(core + jc, NC))

    sibling = fp(0, 1)
    mirror = at(x, y, NZ - 1 - z, core)

    barrier = pltpu.get_barrier_semaphore()
    peers = [zp(j) for j in (4, 3, 5, 2, 6, 1, 7)] + [fp(jz, 1) for jz in (3, 2, 1, 0)]
    peers += [yp(j) for j in range(1, NY)] + [xp(j) for j in range(1, NX)]
    for peer in peers:
        pl.semaphore_signal(barrier, inc=1, device_id=peer, device_id_type=pl.DeviceIdType.MESH)

    LANES = C // 2
    loads = [
        (k_in.at[pl.ds(0, KB)], kv.at[pl.ds(0, KB), pl.ds(0, C)]),
        (v_in.at[pl.ds(0, KB)], kv.at[pl.ds(0, KB), pl.ds(C, C)]),
        (k_in.at[pl.ds(KB, KB)], kv.at[pl.ds(CH, KB), pl.ds(0, C)]),
        (v_in.at[pl.ds(KB, KB)], kv.at[pl.ds(CH, KB), pl.ds(C, C)]),
        (vis_in, vis_i),
        (cnt_in, cnt),
    ]
    for part in range(2):
        lanes = pl.ds(part * LANES, LANES)
        loads += [(q_in.at[:, lanes], qd.at[zh, part, 0]), (g_in.at[:, lanes], qd.at[zh, part, 1])]
    loads = [pltpu.make_async_copy(src, dst, in_s.at[n]) for n, (src, dst) in enumerate(loads)]
    for copy in loads:
        copy.start()
    for copy in loads:
        copy.wait()
    vis[zh, :2, : NX * NZH * NY * 2] = vis_i[...].astype(F32)

    pl.semaphore_wait(barrier, len(peers))

    def rows_to(src, dst, count, sems, j, device):
        return remote(kv.at[pl.ds(src, count)], kv.at[pl.ds(dst, count)], sems[0].at[j - 1], sems[1].at[j - 1], device)

    js = range(1, NX)
    ga1 = [rows_to(0, (NX - j) * KB, KB, (ga1_s, ga1_r), j, xp(j)) for j in js]
    gb1 = [rows_to(CH, CH + (NY - j) * KB, KB, (gb1_s, gb1_r), j, yp(j)) for j in js]
    place = {0: 0, 1: 1, NX - 1: 2, 2: 3}
    ga0 = [rows_to(0, place[NY - j] * 2 * CH, KB, (ga0_s, ga0_r), j, yp(j)) for j in js]
    gb0 = [rows_to(CH, place[NX - j] * 2 * CH + CH, KB, (gb0_s, gb0_r), j, xp(j)) for j in js]
    ga2 = [rows_to(KB, place[NY - j] * 2 * CH + KB, CH - KB, (ga2_s, ga2_r), j, yp(j)) for j in js]
    gb2 = [rows_to(CH + KB, place[NX - j] * 2 * CH + CH + KB, CH - KB, (gb2_s, gb2_r), j, xp(j)) for j in js]
    qx = [remote(qd.at[zh, part, core], qd.at[zh, part, core], qx_s.at[part], qx_r.at[part], mirror) for part in range(2)]
    qc = [remote(qd.at[1 - zh, part, core], qd.at[1 - zh, part, core], qc_s.at[part], qc_r.at[part], sibling) for part in range(2)]
    for copy in ga1 + gb1:
        copy.start()
    qx[0].start()
    qx[1].start()
    vx = remote(vis.at[zh], vis.at[zh], vx_s.at[0], vx_r.at[0], zp(NZL))
    vx.start()
    for copy in ga0 + gb0:
        copy.start()

    head_of = lax.broadcasted_iota(jnp.int32, (QB, LANES), 1) // HD

    def stack(b, part):
        qb = qd[b, part, 0]
        gb = qd[b, part, 1]
        zero = jnp.zeros_like(qb)

        def one(h, _):
            rows = pl.ds(pl.multiple_of((b * H + part * (H // 2) + h) * QB, QB), QB)
            keep = head_of == h
            for ref, block in ((qs, qb), (gs, gb)):
                ref[rows, part * LANES : (part + 1) * LANES] = jnp.where(keep, block, zero)
                ref[rows, (1 - part) * LANES : (2 - part) * LANES] = zero
            return 0

        lax.fori_loop(0, H // 2, one, 0)

    stack(zh, 0)
    stack(zh, 1)

    blocks = NX * NZH * NY * 2
    row = lax.broadcasted_iota(jnp.int32, (KEYS, blocks), 0)
    col = lax.broadcasted_iota(jnp.int32, (KEYS, blocks), 1)
    half = (row % (2 * CH)) // CH
    outer = row // (2 * CH)
    outer = jnp.where(outer == 3, 2, jnp.where(outer == 2, 3, outer))
    inner = (row % CH) // KB
    bx = (x + jnp.where(half == 0, inner, outer)) % NX
    by = (y + jnp.where(half == 0, outer, inner)) % NY
    block = 2 * ((bx * NZH + zh) * NY + by) + half
    pick = ((block == col) & (row % KB < cnt[...])).astype(F32).astype(BF16)

    def cap_of(b):
        seen = jnp.concatenate(
            [jnp.broadcast_to(vis[b, t : t + 1, :blocks], (TQ, blocks)) for t in range(2)], axis=0
        ).astype(BF16)
        cap[b] = jnp.where(nt(pick, seen) > 0.5, BIG, NEG)

    cap_of(zh)

    for one_stage, next_stage in ((ga1, ga2), (gb1, gb2)):
        for copy in one_stage:
            copy.wait_recv()
        for j in (0, 2, 1):
            next_stage[j].start()

    def chunk_rows(i, count=1):
        return pl.ds(i * 2 * CH, count * 2 * CH)

    def first(b, i, count, heads):
        rk = chunk_rows(i, count)
        kc = kv[rk, :C]
        vc = kv[rk, C:]
        for h in heads:
            rows = pl.ds(pl.multiple_of((b * H + h) * QB, QB), QB)
            s = nt(kc, qs[rows, :]) * (SCALE * LOG2E)
            s = jnp.minimum(s, cap[b, rk, :])
            m = jnp.maximum(jnp.max(s, axis=0, keepdims=True), 0.1 * NEG)
            p = jnp.exp2(s - m)
            d = nt(vc, gs[rows, :])
            for u in range(count):
                pbuf[b * NX + i + u, h] = p[u * 2 * CH : (u + 1) * 2 * CH]
                dbuf[b * NX + i + u, h] = d[u * 2 * CH : (u + 1) * 2 * CH]
            group = b * 3 + min(i, 1) + (i == 3)
            cstat[group, 0, h : h + 1, :] = m
            cstat[group, 1, h : h + 1, :] = jnp.sum(p, axis=0, keepdims=True)
            cstat[group, 2, h : h + 1, :] = jnp.sum(p * d, axis=0, keepdims=True)

    def stat_copies(b):
        return [remote(stat.at[b], stat_in.at[b, j - 1], st_s.at[b, j - 1], st_r.at[b, j - 1], zp(j)) for j in range(1, NZ)]

    def stat_send(b):
        parts = [tuple(cstat[b * 3 + i, k] for k in range(3)) for i in range(3)]
        top = parts[0][0]
        for part in parts[1:]:
            top = jnp.maximum(top, part[0])
        total = jnp.zeros_like(top)
        dot = jnp.zeros_like(top)
        for m, l, d in parts:
            w = jnp.exp2(m - top)
            total = total + l * w
            dot = dot + d * w
        total = jnp.maximum(total, 1e-30)
        stat[b, 0] = top + jnp.log2(total)
        stat[b, 1] = dot / total
        copies = stat_copies(b)
        for j in (4, 3, 5, 2, 6, 1, 7):
            copies[j - 1].start()

    def core_copy(b):
        return remote(core_out.at[b], core_in.at[b], sc_s.at[b], sc_r.at[b], sibling)

    def merge(parts):
        top = parts[0][0]
        for part in parts[1:]:
            top = jnp.maximum(top, part[0])
        total = jnp.zeros_like(top)
        dot = jnp.zeros_like(top)
        for lse, mean in parts:
            w = jnp.exp2(lse - top)
            total = total + w
            dot = dot + mean * w
        return top + jnp.log2(total), dot / total

    def stat_ring(b):
        for copy in stat_copies(b):
            copy.wait_recv()
        parts = [(stat[b, 0], stat[b, 1])]
        parts += [(stat_in[b, j, 0], stat_in[b, j, 1]) for j in range(NZ - 1)]
        for k, value in enumerate(merge(parts)):
            core_out[b, k] = value
        core_copy(b).start()

    def stat_final(b):
        core_copy(b).wait_recv()
        lse, mean = merge([(core_out[b, 0], core_out[b, 1]), (core_in[b, 0], core_in[b, 1])])
        for i in range(3):
            alpha[b * 3 + i] = jnp.exp2(cstat[b * 3 + i, 0] - lse)
        delta[b] = mean

    def chunk_copies(i):
        r = {1: 1, 2: NX - 1, 3: 2}[i]
        return (
            remote(rs1_out.at[i - 1, 0], rs1_in.at[r - 1, 0], ra1_s.at[r - 1], ra1_r.at[r - 1], yp(r)),
            remote(rs1_out.at[i - 1, 1], rs1_in.at[r - 1, 1], rb1_s.at[r - 1], rb1_r.at[r - 1], xp(r)),
        )

    def prepare(b, i, slot, first_chunk):
        n = b * NX + i
        group = b * 3 + min(i, 1) + (i == 3)
        dqs = []
        for h in range(H):
            a = alpha[group, h : h + 1, :]
            e = delta[b, h : h + 1, :]
            p = pbuf[n, h] * a
            t = (p * (dbuf[n, h] - e)).astype(BF16)
            pb[slot][:, h * QB : (h + 1) * QB] = p.astype(BF16)
            tb[slot][:, h * QB : (h + 1) * QB] = t
            dqs.append(nn(kt[i, h * HD : (h + 1) * HD, :], t))
        dqc = jnp.concatenate(dqs, axis=0)
        dqt[b] = dqc if first_chunk else dqt[b] + dqc

    def grads(b, i, slot):
        stack_rows = slice(b * H * QB, (b + 1) * H * QB)
        dki = nn(tb[slot][...], qs[stack_rows, :])
        dvi = nn(pb[slot][...], gs[stack_rows, :])
        if b == 1:
            dki = dk[i] + dki
            dvi = dv[i] + dvi
        if b == 0 or i == 0:
            dk[i] = dki
            dv[i] = dvi
            return
        for half in range(2):
            rs1_out[i - 1, half, :, :C] = dki[half * CH : (half + 1) * CH].astype(BF16)
            rs1_out[i - 1, half, :, C:] = dvi[half * CH : (half + 1) * CH].astype(BF16)
        for copy in chunk_copies(i):
            copy.start()

    other_half = pl.ds(pl.multiple_of((1 - core) * QH, QH), QH)

    def dq_core(b):
        return remote(dq.at[b, other_half], dq_sib.at[b], dc_s.at[b], dc_r.at[b], sibling)

    def dq_start(b):
        dq[b] = dqt[b].T * SCALE
        dq_core(b).start()

    def dq_slot(b, j):
        return remote(
            dqz_out.at[b, pl.ds(j * QS, QS)],
            dqz_in.at[z],
            dz_s.at[b * NZL + j],
            dz_r.at[z],
            at(x, y, b * NZL + j, core),
        )

    def dq_ring(b):
        dq_core(b).wait_recv()
        mine = dq[b, pl.ds(pl.multiple_of(core * QH, QH), QH), :] + dq_sib[b]
        dqz_out[b] = mine.astype(BF16)
        for j in range(NZL):

            @pl.when(z == b * NZL + j)
            def _(j=j):
                dqz_own[...] = mine[j * QS : (j + 1) * QS, :]

            @pl.when(z != b * NZL + j)
            def _(j=j):
                dq_slot(b, j).start()

    head_parts = (range(H // 2), range(H // 2, H))
    first(zh, 0, 1, range(H))
    vx.wait_recv()
    cap_of(1 - zh)
    for part, heads in enumerate(head_parts):
        qx[part].wait_recv()
        qc[part].start()
        qc[part].wait_recv()
        stack(1 - zh, part)
        first(1 - zh, 0, 1, heads)

    def shard(b, _):
        @pl.when(b == 0)
        def _():
            for j in (0, 2):
                for copies in (ga0, gb0, ga2, gb2):
                    copies[j].wait_recv()

        first(b, 1, 2, range(H))

        @pl.when(b == 0)
        def _():
            for copies in (ga0, gb0, ga2, gb2):
                copies[1].wait_recv()

        first(b, 3, 1, range(H))
        stat_send(b)
        return 0

    lax.fori_loop(0, NZH, shard, 0)
    for i in range(NX):
        kt[i] = kv[i * 2 * CH : (i + 1) * 2 * CH, :C].astype(F32).T.astype(BF16)
    for copy in ga0 + gb0 + ga1 + gb1 + ga2 + gb2 + qx + qc + [vx]:
        copy.wait_send()
    stat_ring(0)
    stat_final(0)
    steps = [(b, i) for b in range(NZH) for i in (3, 1, 2, 0)]
    prepare(*steps[0], 0, True)
    for k, step in enumerate(steps):
        if k == 2:
            stat_ring(1)
        if k == 3:
            stat_final(1)
        if k + 1 < len(steps):
            prepare(*steps[k + 1], (k + 1) % 2, steps[k + 1][1] == 3)
        grads(*step, k % 2)
        if k == 2:
            dq_start(0)
        if k == 4:
            dq_ring(0)
        if k == 6:
            dq_start(1)

    dq_ring(1)
    def rs2_copies(j):
        rows = pl.ds(j * KB, KB)
        return (
            remote(rs2_out.at[0, rows], rs2_in.at[j - 1, 0], ra2_s.at[j - 1], ra2_r.at[j - 1], xp(j)),
            remote(rs2_out.at[1, rows], rs2_in.at[j - 1, 1], rb2_s.at[j - 1], rb2_r.at[j - 1], yp(j)),
        )

    for half in range(2):
        for r in js:
            chunk_copies(r)[half].wait_recv()
        for part, acc in enumerate((dk, dv)):
            cols = slice(part * C, (part + 1) * C)
            total = acc[0, half * CH : (half + 1) * CH, :]
            for i in range(NX - 1):
                total = total + rs1_in[i, half, :, cols].astype(F32)
            rs2_own[half, :, cols] = total[:KB]
            rs2_out[half, :, cols] = total.astype(BF16)
        for j in (2, 1, 3):
            rs2_copies(j)[half].start()

    total = dqz_own[...]
    for j in range(1, NZ):
        sender = lax.rem(z + j, NZ)
        remote(dqz_out.at[0, pl.ds(0, QS)], dqz_in.at[sender], dz_s.at[0], dz_r.at[sender], sibling).wait_recv()
        total = total + dqz_in[sender].astype(F32)
    dqf_out[...] = total.astype(BF16)

    def dqf_copy(jz, jc):
        k = jz * NC + jc - 1
        return remote(dqf_out, dqf_in.at[k], df_s.at[k], df_r.at[k], fp(jz, jc))

    others = [(jz, jc) for jz in range(NZL) for jc in range(NC) if jz + jc > 0]
    for jz, jc in others:
        dqf_copy(jz, jc).start()
    gq_out[pl.ds(pl.multiple_of(core * QH + zl * QS, QS), QS), :] = dqf_out[...]

    for b in range(NZH):
        for copy in stat_copies(b):
            copy.wait_send()
        core_copy(b).wait_send()
        dq_core(b).wait_send()
        for j in range(NZL):

            @pl.when(z != b * NZL + j)
            def _(b=b, j=j):
                dq_slot(b, j).wait_send()

    for r in js:
        for copy in chunk_copies(r):
            copy.wait_send()
    for j in range(1, NX):
        for copy in rs2_copies(j):
            copy.wait_recv()
    for half in range(2):
        total = rs2_own[half]
        for j in range(NX - 1):
            total = total + rs2_in[j, half].astype(F32)
        gk_out[half * KB : (half + 1) * KB, :] = (total[:, :C] * SCALE).astype(BF16)
        gv_out[half * KB : (half + 1) * KB, :] = total[:, C:].astype(BF16)

    for jz, jc in others:
        dqf_copy(jz, jc).wait_recv()
        fz = lax.rem(zl - jz + NZL, NZL)
        fc = lax.rem(core - jc + NC, NC)
        gq_out[pl.ds(pl.multiple_of(fc * QH + fz * QS, QS), QS), :] = dqf_in[jz * NC + jc - 1]

    for j in js:
        for copy in rs2_copies(j):
            copy.wait_send()
    for jz, jc in others:
        dqf_copy(jz, jc).wait_send()


def write_out(a, b, c, a_out, b_out, c_out, sem):
    copies = [
        pltpu.make_async_copy(src, dst, sem.at[n])
        for n, (src, dst) in enumerate(((a, a_out), (b, b_out), (c, c_out)))
    ]
    for copy in copies:
        copy.start()
    for copy in copies:
        copy.wait()


def shards(queries, keys, values, grad_out, visible, counts):
    vmem = pl.BlockSpec(memory_space=pltpu.VMEM)
    dma = pltpu.SemaphoreType.DMA
    V = pltpu.VMEM
    blocks = NX * NZH * NY * 2
    scratch = [
        V((2, blocks), jnp.int32),
        V((1, blocks), jnp.int32),
        V((2 * CH, H * QB), BF16),
        V((2 * CH, H * QB), BF16),
        V((2 * CH, H * QB), BF16),
        V((2 * CH, H * QB), BF16),
        dma((10,)),
        V((KEYS, 2 * C), BF16),
        V((NZH, 2, 2, QB, C // 2), BF16),
        V((NZH, 8, 128), F32),
        V((NZH * H * QB, C), BF16),
        V((NZH * H * QB, C), BF16),
        V((NZH * NX, H, 2 * CH, QB), F32),
        V((NZH * NX, H, 2 * CH, QB), F32),
        V((NZH, KEYS, QB), F32),
        V((NX, C, 2 * CH), BF16),
        V((NZH * 3, 3, H, QB), F32),
        V((NZH, 2, H, QB), F32),
        V((NZH, NZ - 1, 2, H, QB), F32),
        V((NZH, 2, H, QB), F32),
        V((NZH, 2, H, QB), F32),
        V((NZH * 3, H, QB), F32),
        V((NZH, H, QB), F32),
        V((NX, 2 * CH, C), F32),
        V((NX, 2 * CH, C), F32),
        V((NX - 1, 2, CH, 2 * C), BF16),
        V((NX - 1, 2, CH, 2 * C), BF16),
        V((2, KB, 2 * C), F32),
        V((2, CH, 2 * C), BF16),
        V((NX - 1, 2, KB, 2 * C), BF16),
        V((NZH, C, QB), F32),
        V((NZH, QB, C), F32),
        V((NZH, QH, C), F32),
        V((QS, C), F32),
        V((NZH, QH, C), BF16),
        V((NZ, QS, C), BF16),
        V((QS, C), BF16),
        V((NZL * NC - 1, QS, C), BF16),
    ]
    sems = [(NX - 1,)] * 12 + [(2,)] * 6 + [(NZH, NZ - 1)] * 2 + [(NZH,)] * 2 + [(NX - 1,)] * 8
    sems += [(NZH,)] * 2 + [(NZ,)] * 2 + [(NZL * NC - 1,)] * 2
    scratch += [dma(s) for s in sems]
    shapes = [(QB, C), (2 * KB, C), (2 * KB, C)]
    anywhere = pl.BlockSpec(memory_space=pl.ANY)
    grads = pl.pallas_call(
        kernel,
        out_shape=tuple(pltpu.VMEM(s, BF16) for s in shapes),
        in_specs=[anywhere] * 6,
        out_specs=(vmem,) * 3,
        scratch_shapes=scratch,
        compiler_params=pltpu.CompilerParams(
            collective_id=0, has_side_effects=True, vmem_limit_bytes=62 * 1024 * 1024
        ),
    )(queries, grad_out, keys, values, visible, counts.reshape(1, -1))
    grads = [pltpu.with_memory_space_constraint(g, pltpu.VMEM) for g in grads]
    return pl.pallas_call(
        write_out,
        out_shape=tuple(jax.ShapeDtypeStruct(s, BF16) for s in shapes),
        in_specs=[vmem] * 3,
        out_specs=(anywhere,) * 3,
        scratch_shapes=[dma((3,))],
    )(*grads)


def solution(mesh):
    in_specs = (
        P("tile", None),
        P(("cam", "tile"), None),
        P(("cam", "tile"), None),
        P("tile", None),
        P("tile", "cam"),
        P("cam"),
    )
    out_specs = (P("tile", None), P(("cam", "tile"), None), P(("cam", "tile"), None))
    return jax.shard_map(shards, mesh=mesh, in_specs=in_specs, out_specs=out_specs, check_vma=False)
```

```python
import math

import jax
import jax.numpy as jnp
from jax import lax
from jax.experimental import pallas as pl
from jax.experimental.pallas import tpu as pltpu
from jax.sharding import PartitionSpec as P

NX, NY, NZH, NZL, NC = 4, 4, 2, 4, 2
NZ = NZH * NZL
H = 8
HD = 32
C = H * HD
KB = 32
TQ = 128
NEG = -1e30
BIG = 3e38
SCALE = 1.0 / math.sqrt(HD)
LOG2E = math.log2(math.e)
CH = KB * NX
KEYS = 2 * NY * CH
HALF = KEYS // 2
QB = 2 * TQ
QH = QB // NC
QS = QH // NZL

F32 = jnp.float32
BF16 = jnp.bfloat16


def nt(a, b):
    return lax.dot_general(a, b, (((1,), (1,)), ((), ())), preferred_element_type=F32)


def nn(a, b):
    return jnp.dot(a, b, preferred_element_type=F32)


def remote(src, dst, send, recv, device):
    return pltpu.make_async_remote_copy(
        src_ref=src,
        dst_ref=dst,
        send_sem=send,
        recv_sem=recv,
        device_id=device,
        device_id_type=pl.DeviceIdType.MESH,
    )


def kernel(
    q_in, g_in, k_in, v_in, vis_in, cnt_in,
    gq_out, gk_out, gv_out,
    vis_i, cnt, pb_0, pb_1, tb_0, tb_1, in_s, kv, qd, vis, qs, gs, pbuf, dbuf, cap, kt,
    cstat, stat, stat_in, core_out, core_in, alpha, delta,
    dk, dv, rs1_out, rs1_in, rs2_own, rs2_out, rs2_in,
    dqt, dq, dq_sib, dqz_own, dqz_out, dqz_in, dqf_out, dqf_in,
    ga0_s, ga0_r, gb0_s, gb0_r, ga1_s, ga1_r, gb1_s, gb1_r, ga2_s, ga2_r, gb2_s, gb2_r,
    qx_s, qx_r, qc_s, qc_r, vx_s, vx_r,
    st_s, st_r, sc_s, sc_r,
    ra1_s, ra1_r, rb1_s, rb1_r, ra2_s, ra2_r, rb2_s, rb2_r,
    dc_s, dc_r, dz_s, dz_r, df_s, df_r,
):
    pb = (pb_0, pb_1)
    tb = (tb_0, tb_1)
    cam = lax.axis_index("cam")
    tile = lax.axis_index("tile")
    core = lax.rem(cam, NC)
    zl = lax.div(cam, NC)
    y = lax.rem(tile, NY)
    zh = lax.rem(lax.div(tile, NY), NZH)
    x = lax.div(tile, NY * NZH)
    z = zh * NZL + zl

    def at(x_, y_, z_, core_):
        zh_ = lax.div(z_, NZL)
        zl_ = lax.rem(z_, NZL)
        return {"cam": zl_ * NC + core_, "tile": (x_ * NZH + zh_) * NY + y_}

    def xp(j):
        return at(lax.rem(x + j, NX), y, z, core)

    def yp(j):
        return at(x, lax.rem(y + j, NY), z, core)

    def zp(j):
        return at(x, y, lax.rem(z + j, NZ), core)

    def fp(jz, jc):
        return at(x, y, zh * NZL + lax.rem(zl + jz, NZL), lax.rem(core + jc, NC))

    sibling = fp(0, 1)
    mirror = at(x, y, NZ - 1 - z, core)

    barrier = pltpu.get_barrier_semaphore()
    peers = [zp(j) for j in (4, 3, 5, 2, 6, 1, 7)] + [fp(jz, 1) for jz in (3, 2, 1, 0)]
    peers += [yp(j) for j in range(1, NY)] + [xp(j) for j in range(1, NX)]
    for peer in peers:
        pl.semaphore_signal(barrier, inc=1, device_id=peer, device_id_type=pl.DeviceIdType.MESH)

    LANES = C // 2
    loads = [
        (k_in.at[pl.ds(0, KB)], kv.at[pl.ds(0, KB), pl.ds(0, C)]),
        (v_in.at[pl.ds(0, KB)], kv.at[pl.ds(0, KB), pl.ds(C, C)]),
        (k_in.at[pl.ds(KB, KB)], kv.at[pl.ds(CH, KB), pl.ds(0, C)]),
        (v_in.at[pl.ds(KB, KB)], kv.at[pl.ds(CH, KB), pl.ds(C, C)]),
        (vis_in, vis_i),
        (cnt_in, cnt),
    ]
    for part in range(2):
        lanes = pl.ds(part * LANES, LANES)
        loads += [(q_in.at[:, lanes], qd.at[zh, part, 0]), (g_in.at[:, lanes], qd.at[zh, part, 1])]
    loads = [pltpu.make_async_copy(src, dst, in_s.at[n]) for n, (src, dst) in enumerate(loads)]
    for copy in loads:
        copy.start()
    for copy in loads:
        copy.wait()
    vis[zh, :2, : NX * NZH * NY * 2] = vis_i[...].astype(F32)

    pl.semaphore_wait(barrier, len(peers))

    def rows_to(src, dst, count, sems, j, device):
        return remote(kv.at[pl.ds(src, count)], kv.at[pl.ds(dst, count)], sems[0].at[j - 1], sems[1].at[j - 1], device)

    js = range(1, NX)
    ga1 = [rows_to(0, (NX - j) * KB, KB, (ga1_s, ga1_r), j, xp(j)) for j in js]
    gb1 = [rows_to(CH, CH + (NY - j) * KB, KB, (gb1_s, gb1_r), j, yp(j)) for j in js]
    place = {0: 0, 1: 1, NX - 1: 2, 2: 3}
    ga0 = [rows_to(0, place[NY - j] * 2 * CH, KB, (ga0_s, ga0_r), j, yp(j)) for j in js]
    gb0 = [rows_to(CH, place[NX - j] * 2 * CH + CH, KB, (gb0_s, gb0_r), j, xp(j)) for j in js]
    ga2 = [rows_to(KB, place[NY - j] * 2 * CH + KB, CH - KB, (ga2_s, ga2_r), j, yp(j)) for j in js]
    gb2 = [rows_to(CH + KB, place[NX - j] * 2 * CH + CH + KB, CH - KB, (gb2_s, gb2_r), j, xp(j)) for j in js]
    qx = [remote(qd.at[zh, part, core], qd.at[zh, part, core], qx_s.at[part], qx_r.at[part], mirror) for part in range(2)]
    qc = [remote(qd.at[1 - zh, part, core], qd.at[1 - zh, part, core], qc_s.at[part], qc_r.at[part], sibling) for part in range(2)]
    for copy in ga1 + gb1:
        copy.start()
    qx[0].start()
    qx[1].start()
    vx = remote(vis.at[zh], vis.at[zh], vx_s.at[0], vx_r.at[0], zp(NZL))
    vx.start()
    for copy in ga0 + gb0:
        copy.start()

    head_of = lax.broadcasted_iota(jnp.int32, (QB, LANES), 1) // HD

    def stack(b, part):
        qb = qd[b, part, 0]
        gb = qd[b, part, 1]
        zero = jnp.zeros_like(qb)

        def one(h, _):
            rows = pl.ds(pl.multiple_of((b * H + part * (H // 2) + h) * QB, QB), QB)
            keep = head_of == h
            for ref, block in ((qs, qb), (gs, gb)):
                ref[rows, part * LANES : (part + 1) * LANES] = jnp.where(keep, block, zero)
                ref[rows, (1 - part) * LANES : (2 - part) * LANES] = zero
            return 0

        lax.fori_loop(0, H // 2, one, 0)

    stack(zh, 0)
    stack(zh, 1)

    blocks = NX * NZH * NY * 2
    row = lax.broadcasted_iota(jnp.int32, (KEYS, blocks), 0)
    col = lax.broadcasted_iota(jnp.int32, (KEYS, blocks), 1)
    half = (row % (2 * CH)) // CH
    outer = row // (2 * CH)
    outer = jnp.where(outer == 3, 2, jnp.where(outer == 2, 3, outer))
    inner = (row % CH) // KB
    bx = (x + jnp.where(half == 0, inner, outer)) % NX
    by = (y + jnp.where(half == 0, outer, inner)) % NY
    block = 2 * ((bx * NZH + zh) * NY + by) + half
    pick = ((block == col) & (row % KB < cnt[...])).astype(F32).astype(BF16)

    def cap_of(b):
        seen = jnp.concatenate(
            [jnp.broadcast_to(vis[b, t : t + 1, :blocks], (TQ, blocks)) for t in range(2)], axis=0
        ).astype(BF16)
        cap[b] = jnp.where(nt(pick, seen) > 0.5, BIG, NEG)

    cap_of(zh)

    for one_stage, next_stage in ((ga1, ga2), (gb1, gb2)):
        for copy in one_stage:
            copy.wait_recv()
        for j in (0, 2, 1):
            next_stage[j].start()

    def chunk_rows(i, count=1):
        return pl.ds(i * 2 * CH, count * 2 * CH)

    def first(b, i, count, heads):
        rk = chunk_rows(i, count)
        kc = kv[rk, :C]
        vc = kv[rk, C:]
        for h in heads:
            rows = pl.ds(pl.multiple_of((b * H + h) * QB, QB), QB)
            s = nt(kc, qs[rows, :]) * (SCALE * LOG2E)
            s = jnp.minimum(s, cap[b, rk, :])
            m = jnp.maximum(jnp.max(s, axis=0, keepdims=True), 0.1 * NEG)
            p = jnp.exp2(s - m)
            d = nt(vc, gs[rows, :])
            for u in range(count):
                pbuf[b * NX + i + u, h] = p[u * 2 * CH : (u + 1) * 2 * CH]
                dbuf[b * NX + i + u, h] = d[u * 2 * CH : (u + 1) * 2 * CH]
            group = b * 3 + min(i, 1) + (i == 3)
            cstat[group, 0, h : h + 1, :] = m
            cstat[group, 1, h : h + 1, :] = jnp.sum(p, axis=0, keepdims=True)
            cstat[group, 2, h : h + 1, :] = jnp.sum(p * d, axis=0, keepdims=True)

    def stat_copies(b):
        return [remote(stat.at[b], stat_in.at[b, j - 1], st_s.at[b, j - 1], st_r.at[b, j - 1], zp(j)) for j in range(1, NZ)]

    def stat_send(b):
        parts = [tuple(cstat[b * 3 + i, k] for k in range(3)) for i in range(3)]
        top = parts[0][0]
        for part in parts[1:]:
            top = jnp.maximum(top, part[0])
        total = jnp.zeros_like(top)
        dot = jnp.zeros_like(top)
        for m, l, d in parts:
            w = jnp.exp2(m - top)
            total = total + l * w
            dot = dot + d * w
        total = jnp.maximum(total, 1e-30)
        stat[b, 0] = top + jnp.log2(total)
        stat[b, 1] = dot / total
        copies = stat_copies(b)
        for j in (4, 3, 5, 2, 6, 1, 7):
            copies[j - 1].start()

    def core_copy(b):
        return remote(core_out.at[b], core_in.at[b], sc_s.at[b], sc_r.at[b], sibling)

    def merge(parts):
        top = parts[0][0]
        for part in parts[1:]:
            top = jnp.maximum(top, part[0])
        total = jnp.zeros_like(top)
        dot = jnp.zeros_like(top)
        for lse, mean in parts:
            w = jnp.exp2(lse - top)
            total = total + w
            dot = dot + mean * w
        return top + jnp.log2(total), dot / total

    def stat_ring(b):
        for copy in stat_copies(b):
            copy.wait_recv()
        parts = [(stat[b, 0], stat[b, 1])]
        parts += [(stat_in[b, j, 0], stat_in[b, j, 1]) for j in range(NZ - 1)]
        for k, value in enumerate(merge(parts)):
            core_out[b, k] = value
        core_copy(b).start()

    def stat_final(b):
        core_copy(b).wait_recv()
        lse, mean = merge([(core_out[b, 0], core_out[b, 1]), (core_in[b, 0], core_in[b, 1])])
        for i in range(3):
            alpha[b * 3 + i] = jnp.exp2(cstat[b * 3 + i, 0] - lse)
        delta[b] = mean

    def chunk_copies(i):
        r = {1: 1, 2: NX - 1, 3: 2}[i]
        return (
            remote(rs1_out.at[i - 1, 0], rs1_in.at[r - 1, 0], ra1_s.at[r - 1], ra1_r.at[r - 1], yp(r)),
            remote(rs1_out.at[i - 1, 1], rs1_in.at[r - 1, 1], rb1_s.at[r - 1], rb1_r.at[r - 1], xp(r)),
        )

    def prepare(b, i, slot, first_chunk):
        n = b * NX + i
        group = b * 3 + min(i, 1) + (i == 3)
        dqs = []
        for h in range(H):
            a = alpha[group, h : h + 1, :]
            e = delta[b, h : h + 1, :]
            p = pbuf[n, h] * a
            t = (p * (dbuf[n, h] - e)).astype(BF16)
            pb[slot][:, h * QB : (h + 1) * QB] = p.astype(BF16)
            tb[slot][:, h * QB : (h + 1) * QB] = t
            dqs.append(nn(kt[i, h * HD : (h + 1) * HD, :], t))
        dqc = jnp.concatenate(dqs, axis=0)
        dqt[b] = dqc if first_chunk else dqt[b] + dqc

    def grads(b, i, slot):
        stack_rows = slice(b * H * QB, (b + 1) * H * QB)
        dki = nn(tb[slot][...], qs[stack_rows, :])
        dvi = nn(pb[slot][...], gs[stack_rows, :])
        if b == 1:
            dki = dk[i] + dki
            dvi = dv[i] + dvi
        if b == 0 or i == 0:
            dk[i] = dki
            dv[i] = dvi
            return
        for half in range(2):
            rs1_out[i - 1, half, :, :C] = dki[half * CH : (half + 1) * CH].astype(BF16)
            rs1_out[i - 1, half, :, C:] = dvi[half * CH : (half + 1) * CH].astype(BF16)
        for copy in chunk_copies(i):
            copy.start()

    other_half = pl.ds(pl.multiple_of((1 - core) * QH, QH), QH)

    def dq_core(b):
        return remote(dq.at[b, other_half], dq_sib.at[b], dc_s.at[b], dc_r.at[b], sibling)

    def dq_start(b):
        dq[b] = dqt[b].T * SCALE
        dq_core(b).start()

    def dq_slot(b, j):
        return remote(
            dqz_out.at[b, pl.ds(j * QS, QS)],
            dqz_in.at[z],
            dz_s.at[b * NZL + j],
            dz_r.at[z],
            at(x, y, b * NZL + j, core),
        )

    def dq_ring(b):
        dq_core(b).wait_recv()
        mine = dq[b, pl.ds(pl.multiple_of(core * QH, QH), QH), :] + dq_sib[b]
        dqz_out[b] = mine.astype(BF16)
        for j in range(NZL):

            @pl.when(z == b * NZL + j)
            def _(j=j):
                dqz_own[...] = mine[j * QS : (j + 1) * QS, :]

            @pl.when(z != b * NZL + j)
            def _(j=j):
                dq_slot(b, j).start()

    head_parts = (range(H // 2), range(H // 2, H))
    first(zh, 0, 1, range(H))
    qx[0].wait_recv()
    qc[0].start()
    vx.wait_recv()
    cap_of(1 - zh)
    qc[0].wait_recv()
    stack(1 - zh, 0)
    qx[1].wait_recv()
    qc[1].start()
    first(1 - zh, 0, 1, head_parts[0])
    qc[1].wait_recv()
    stack(1 - zh, 1)
    first(1 - zh, 0, 1, head_parts[1])

    def shard(b, _):
        @pl.when(b == 0)
        def _():
            for j in (0, 2):
                for copies in (ga0, gb0, ga2, gb2):
                    copies[j].wait_recv()

        first(b, 1, 2, range(H))

        @pl.when(b == 0)
        def _():
            for copies in (ga0, gb0, ga2, gb2):
                copies[1].wait_recv()

        first(b, 3, 1, range(H))
        stat_send(b)
        return 0

    lax.fori_loop(0, NZH, shard, 0)
    for i in range(NX):
        kt[i] = kv[i * 2 * CH : (i + 1) * 2 * CH, :C].astype(F32).T.astype(BF16)
    for copy in ga0 + gb0 + ga1 + gb1 + ga2 + gb2 + qx + qc + [vx]:
        copy.wait_send()
    stat_ring(0)
    stat_final(0)
    steps = [(b, i) for b in range(NZH) for i in (3, 1, 2, 0)]
    prepare(*steps[0], 0, True)
    for k, step in enumerate(steps):
        if k == 2:
            stat_ring(1)
        if k == 3:
            stat_final(1)
        if k + 1 < len(steps):
            prepare(*steps[k + 1], (k + 1) % 2, steps[k + 1][1] == 3)
        grads(*step, k % 2)
        if k == 2:
            dq_start(0)
        if k == 4:
            dq_ring(0)
        if k == 6:
            dq_start(1)

    dq_ring(1)
    def rs2_copies(j):
        rows = pl.ds(j * KB, KB)
        return (
            remote(rs2_out.at[0, rows], rs2_in.at[j - 1, 0], ra2_s.at[j - 1], ra2_r.at[j - 1], xp(j)),
            remote(rs2_out.at[1, rows], rs2_in.at[j - 1, 1], rb2_s.at[j - 1], rb2_r.at[j - 1], yp(j)),
        )

    for half in range(2):
        for r in js:
            chunk_copies(r)[half].wait_recv()
        for part, acc in enumerate((dk, dv)):
            cols = slice(part * C, (part + 1) * C)
            total = acc[0, half * CH : (half + 1) * CH, :]
            for i in range(NX - 1):
                total = total + rs1_in[i, half, :, cols].astype(F32)
            rs2_own[half, :, cols] = total[:KB]
            rs2_out[half, :, cols] = total.astype(BF16)
        for j in (2, 1, 3):
            rs2_copies(j)[half].start()

    total = dqz_own[...]
    for j in range(1, NZ):
        sender = lax.rem(z + j, NZ)
        remote(dqz_out.at[0, pl.ds(0, QS)], dqz_in.at[sender], dz_s.at[0], dz_r.at[sender], sibling).wait_recv()
        total = total + dqz_in[sender].astype(F32)
    dqf_out[...] = total.astype(BF16)

    def dqf_copy(jz, jc):
        k = jz * NC + jc - 1
        return remote(dqf_out, dqf_in.at[k], df_s.at[k], df_r.at[k], fp(jz, jc))

    others = [(jz, jc) for jz in range(NZL) for jc in range(NC) if jz + jc > 0]
    for jz, jc in others:
        dqf_copy(jz, jc).start()
    gq_out[pl.ds(pl.multiple_of(core * QH + zl * QS, QS), QS), :] = dqf_out[...]

    for b in range(NZH):
        for copy in stat_copies(b):
            copy.wait_send()
        core_copy(b).wait_send()
        dq_core(b).wait_send()
        for j in range(NZL):

            @pl.when(z != b * NZL + j)
            def _(b=b, j=j):
                dq_slot(b, j).wait_send()

    for r in js:
        for copy in chunk_copies(r):
            copy.wait_send()
    for j in range(1, NX):
        for copy in rs2_copies(j):
            copy.wait_recv()
    for half in range(2):
        total = rs2_own[half]
        for j in range(NX - 1):
            total = total + rs2_in[j, half].astype(F32)
        gk_out[half * KB : (half + 1) * KB, :] = (total[:, :C] * SCALE).astype(BF16)
        gv_out[half * KB : (half + 1) * KB, :] = total[:, C:].astype(BF16)

    for jz, jc in others:
        dqf_copy(jz, jc).wait_recv()
        fz = lax.rem(zl - jz + NZL, NZL)
        fc = lax.rem(core - jc + NC, NC)
        gq_out[pl.ds(pl.multiple_of(fc * QH + fz * QS, QS), QS), :] = dqf_in[jz * NC + jc - 1]

    for j in js:
        for copy in rs2_copies(j):
            copy.wait_send()
    for jz, jc in others:
        dqf_copy(jz, jc).wait_send()


def write_out(a, b, c, a_out, b_out, c_out, sem):
    copies = [
        pltpu.make_async_copy(src, dst, sem.at[n])
        for n, (src, dst) in enumerate(((a, a_out), (b, b_out), (c, c_out)))
    ]
    for copy in copies:
        copy.start()
    for copy in copies:
        copy.wait()


def shards(queries, keys, values, grad_out, visible, counts):
    vmem = pl.BlockSpec(memory_space=pltpu.VMEM)
    dma = pltpu.SemaphoreType.DMA
    V = pltpu.VMEM
    blocks = NX * NZH * NY * 2
    scratch = [
        V((2, blocks), jnp.int32),
        V((1, blocks), jnp.int32),
        V((2 * CH, H * QB), BF16),
        V((2 * CH, H * QB), BF16),
        V((2 * CH, H * QB), BF16),
        V((2 * CH, H * QB), BF16),
        dma((10,)),
        V((KEYS, 2 * C), BF16),
        V((NZH, 2, 2, QB, C // 2), BF16),
        V((NZH, 8, 128), F32),
        V((NZH * H * QB, C), BF16),
        V((NZH * H * QB, C), BF16),
        V((NZH * NX, H, 2 * CH, QB), F32),
        V((NZH * NX, H, 2 * CH, QB), F32),
        V((NZH, KEYS, QB), F32),
        V((NX, C, 2 * CH), BF16),
        V((NZH * 3, 3, H, QB), F32),
        V((NZH, 2, H, QB), F32),
        V((NZH, NZ - 1, 2, H, QB), F32),
        V((NZH, 2, H, QB), F32),
        V((NZH, 2, H, QB), F32),
        V((NZH * 3, H, QB), F32),
        V((NZH, H, QB), F32),
        V((NX, 2 * CH, C), F32),
        V((NX, 2 * CH, C), F32),
        V((NX - 1, 2, CH, 2 * C), BF16),
        V((NX - 1, 2, CH, 2 * C), BF16),
        V((2, KB, 2 * C), F32),
        V((2, CH, 2 * C), BF16),
        V((NX - 1, 2, KB, 2 * C), BF16),
        V((NZH, C, QB), F32),
        V((NZH, QB, C), F32),
        V((NZH, QH, C), F32),
        V((QS, C), F32),
        V((NZH, QH, C), BF16),
        V((NZ, QS, C), BF16),
        V((QS, C), BF16),
        V((NZL * NC - 1, QS, C), BF16),
    ]
    sems = [(NX - 1,)] * 12 + [(2,)] * 6 + [(NZH, NZ - 1)] * 2 + [(NZH,)] * 2 + [(NX - 1,)] * 8
    sems += [(NZH,)] * 2 + [(NZ,)] * 2 + [(NZL * NC - 1,)] * 2
    scratch += [dma(s) for s in sems]
    shapes = [(QB, C), (2 * KB, C), (2 * KB, C)]
    anywhere = pl.BlockSpec(memory_space=pl.ANY)
    grads = pl.pallas_call(
        kernel,
        out_shape=tuple(pltpu.VMEM(s, BF16) for s in shapes),
        in_specs=[anywhere] * 6,
        out_specs=(vmem,) * 3,
        scratch_shapes=scratch,
        compiler_params=pltpu.CompilerParams(
            collective_id=0, has_side_effects=True, vmem_limit_bytes=62 * 1024 * 1024
        ),
    )(queries, grad_out, keys, values, visible, counts.reshape(1, -1))
    grads = [pltpu.with_memory_space_constraint(g, pltpu.VMEM) for g in grads]
    return pl.pallas_call(
        write_out,
        out_shape=tuple(jax.ShapeDtypeStruct(s, BF16) for s in shapes),
        in_specs=[vmem] * 3,
        out_specs=(anywhere,) * 3,
        scratch_shapes=[dma((3,))],
    )(*grads)


def solution(mesh):
    in_specs = (
        P("tile", None),
        P(("cam", "tile"), None),
        P(("cam", "tile"), None),
        P("tile", None),
        P("tile", "cam"),
        P("cam"),
    )
    out_specs = (P("tile", None), P(("cam", "tile"), None), P(("cam", "tile"), None))
    return jax.shard_map(shards, mesh=mesh, in_specs=in_specs, out_specs=out_specs, check_vma=False)
```

```python
import math

import jax
import jax.numpy as jnp
from jax import lax
from jax.experimental import pallas as pl
from jax.experimental.pallas import tpu as pltpu
from jax.sharding import PartitionSpec as P

NX, NY, NZH, NZL, NC = 4, 4, 2, 4, 2
NZ = NZH * NZL
H = 8
HD = 32
C = H * HD
KB = 32
TQ = 128
NEG = -1e30
BIG = 3e38
SCALE = 1.0 / math.sqrt(HD)
LOG2E = math.log2(math.e)
CH = KB * NX
KEYS = 2 * NY * CH
HALF = KEYS // 2
QB = 2 * TQ
QH = QB // NC
QS = QH // NZL

F32 = jnp.float32
BF16 = jnp.bfloat16


def nt(a, b):
    return lax.dot_general(a, b, (((1,), (1,)), ((), ())), preferred_element_type=F32)


def nn(a, b):
    return jnp.dot(a, b, preferred_element_type=F32)


def remote(src, dst, send, recv, device):
    return pltpu.make_async_remote_copy(
        src_ref=src,
        dst_ref=dst,
        send_sem=send,
        recv_sem=recv,
        device_id=device,
        device_id_type=pl.DeviceIdType.MESH,
    )


def kernel(
    q_in, g_in, k_in, v_in, vis_in, cnt_in,
    gq_out, gk_out, gv_out,
    vis_i, cnt, pb_0, pb_1, tb_0, tb_1, in_s, kv, qd, vis, qs, gs, pbuf, dbuf, cap, kt,
    cstat, stat, stat_in, core_out, core_in, alpha, delta,
    dk, dv, rs1_out, rs1_in, rs2_own, rs2_out, rs2_in,
    dqt, dq, dq_sib, dqz_own, dqz_out, dqz_in, dqf_out, dqf_in,
    ga0_s, ga0_r, gb0_s, gb0_r, ga1_s, ga1_r, gb1_s, gb1_r, ga2_s, ga2_r, gb2_s, gb2_r,
    qx_s, qx_r, qc_s, qc_r, vx_s, vx_r,
    st_s, st_r, sc_s, sc_r,
    ra1_s, ra1_r, rb1_s, rb1_r, ra2_s, ra2_r, rb2_s, rb2_r,
    dc_s, dc_r, dz_s, dz_r, df_s, df_r,
):
    pb = (pb_0, pb_1)
    tb = (tb_0, tb_1)
    cam = lax.axis_index("cam")
    tile = lax.axis_index("tile")
    core = lax.rem(cam, NC)
    zl = lax.div(cam, NC)
    y = lax.rem(tile, NY)
    zh = lax.rem(lax.div(tile, NY), NZH)
    x = lax.div(tile, NY * NZH)
    z = zh * NZL + zl

    def at(x_, y_, z_, core_):
        zh_ = lax.div(z_, NZL)
        zl_ = lax.rem(z_, NZL)
        return {"cam": zl_ * NC + core_, "tile": (x_ * NZH + zh_) * NY + y_}

    def xp(j):
        return at(lax.rem(x + j, NX), y, z, core)

    def yp(j):
        return at(x, lax.rem(y + j, NY), z, core)

    def zp(j):
        return at(x, y, lax.rem(z + j, NZ), core)

    def fp(jz, jc):
        return at(x, y, zh * NZL + lax.rem(zl + jz, NZL), lax.rem(core + jc, NC))

    sibling = fp(0, 1)
    mirror = at(x, y, NZ - 1 - z, core)

    barrier = pltpu.get_barrier_semaphore()
    peers = [zp(j) for j in (4, 3, 5, 2, 6, 1, 7)] + [fp(jz, 1) for jz in (3, 2, 1, 0)]
    peers += [yp(j) for j in range(1, NY)] + [xp(j) for j in range(1, NX)]
    for peer in peers:
        pl.semaphore_signal(barrier, inc=1, device_id=peer, device_id_type=pl.DeviceIdType.MESH)

    LANES = C // 2
    loads = [
        (k_in.at[pl.ds(0, KB)], kv.at[pl.ds(0, KB), pl.ds(0, C)]),
        (v_in.at[pl.ds(0, KB)], kv.at[pl.ds(0, KB), pl.ds(C, C)]),
        (k_in.at[pl.ds(KB, KB)], kv.at[pl.ds(CH, KB), pl.ds(0, C)]),
        (v_in.at[pl.ds(KB, KB)], kv.at[pl.ds(CH, KB), pl.ds(C, C)]),
        (vis_in, vis_i),
        (cnt_in, cnt),
    ]
    for part in range(2):
        lanes = pl.ds(part * LANES, LANES)
        loads += [(q_in.at[:, lanes], qd.at[zh, part, 0]), (g_in.at[:, lanes], qd.at[zh, part, 1])]
    loads = [pltpu.make_async_copy(src, dst, in_s.at[n]) for n, (src, dst) in enumerate(loads)]
    for copy in loads:
        copy.start()
    for copy in loads:
        copy.wait()
    vis[zh, :2, : NX * NZH * NY * 2] = vis_i[...].astype(F32)

    pl.semaphore_wait(barrier, len(peers))

    def rows_to(src, dst, count, sems, j, device):
        return remote(kv.at[pl.ds(src, count)], kv.at[pl.ds(dst, count)], sems[0].at[j - 1], sems[1].at[j - 1], device)

    js = range(1, NX)
    ga1 = [rows_to(0, (NX - j) * KB, KB, (ga1_s, ga1_r), j, xp(j)) for j in js]
    gb1 = [rows_to(CH, CH + (NY - j) * KB, KB, (gb1_s, gb1_r), j, yp(j)) for j in js]
    place = {0: 0, 1: 1, NX - 1: 2, 2: 3}
    ga0 = [rows_to(0, place[NY - j] * 2 * CH, KB, (ga0_s, ga0_r), j, yp(j)) for j in js]
    gb0 = [rows_to(CH, place[NX - j] * 2 * CH + CH, KB, (gb0_s, gb0_r), j, xp(j)) for j in js]
    ga2 = [rows_to(KB, place[NY - j] * 2 * CH + KB, CH - KB, (ga2_s, ga2_r), j, yp(j)) for j in js]
    gb2 = [rows_to(CH + KB, place[NX - j] * 2 * CH + CH + KB, CH - KB, (gb2_s, gb2_r), j, xp(j)) for j in js]
    qx = [remote(qd.at[zh, part, core], qd.at[zh, part, core], qx_s.at[part], qx_r.at[part], mirror) for part in range(2)]
    qc = [remote(qd.at[1 - zh, part, core], qd.at[1 - zh, part, core], qc_s.at[part], qc_r.at[part], sibling) for part in range(2)]
    qx[0].start()
    qx[1].start()
    for copy in ga1 + gb1:
        copy.start()
    vx = remote(vis.at[zh], vis.at[zh], vx_s.at[0], vx_r.at[0], zp(NZL))
    vx.start()
    for copy in ga0 + gb0:
        copy.start()

    head_of = lax.broadcasted_iota(jnp.int32, (QB, LANES), 1) // HD

    def stack(b, part):
        qb = qd[b, part, 0]
        gb = qd[b, part, 1]
        zero = jnp.zeros_like(qb)

        def one(h, _):
            rows = pl.ds(pl.multiple_of((b * H + part * (H // 2) + h) * QB, QB), QB)
            keep = head_of == h
            for ref, block in ((qs, qb), (gs, gb)):
                ref[rows, part * LANES : (part + 1) * LANES] = jnp.where(keep, block, zero)
                ref[rows, (1 - part) * LANES : (2 - part) * LANES] = zero
            return 0

        lax.fori_loop(0, H // 2, one, 0)

    stack(zh, 0)
    stack(zh, 1)

    blocks = NX * NZH * NY * 2
    row = lax.broadcasted_iota(jnp.int32, (KEYS, blocks), 0)
    col = lax.broadcasted_iota(jnp.int32, (KEYS, blocks), 1)
    half = (row % (2 * CH)) // CH
    outer = row // (2 * CH)
    outer = jnp.where(outer == 3, 2, jnp.where(outer == 2, 3, outer))
    inner = (row % CH) // KB
    bx = (x + jnp.where(half == 0, inner, outer)) % NX
    by = (y + jnp.where(half == 0, outer, inner)) % NY
    block = 2 * ((bx * NZH + zh) * NY + by) + half
    pick = ((block == col) & (row % KB < cnt[...])).astype(F32).astype(BF16)

    def cap_of(b):
        seen = jnp.concatenate(
            [jnp.broadcast_to(vis[b, t : t + 1, :blocks], (TQ, blocks)) for t in range(2)], axis=0
        ).astype(BF16)
        cap[b] = jnp.where(nt(pick, seen) > 0.5, BIG, NEG)

    cap_of(zh)

    for one_stage, next_stage in ((ga1, ga2), (gb1, gb2)):
        for copy in one_stage:
            copy.wait_recv()
        for j in (0, 2, 1):
            next_stage[j].start()

    def chunk_rows(i, count=1):
        return pl.ds(i * 2 * CH, count * 2 * CH)

    def first(b, i, count, heads):
        rk = chunk_rows(i, count)
        kc = kv[rk, :C]
        vc = kv[rk, C:]
        for h in heads:
            rows = pl.ds(pl.multiple_of((b * H + h) * QB, QB), QB)
            s = nt(kc, qs[rows, :]) * (SCALE * LOG2E)
            s = jnp.minimum(s, cap[b, rk, :])
            m = jnp.maximum(jnp.max(s, axis=0, keepdims=True), 0.1 * NEG)
            p = jnp.exp2(s - m)
            d = nt(vc, gs[rows, :])
            for u in range(count):
                pbuf[b * NX + i + u, h] = p[u * 2 * CH : (u + 1) * 2 * CH]
                dbuf[b * NX + i + u, h] = d[u * 2 * CH : (u + 1) * 2 * CH]
            group = b * 3 + min(i, 1) + (i == 3)
            cstat[group, 0, h : h + 1, :] = m
            cstat[group, 1, h : h + 1, :] = jnp.sum(p, axis=0, keepdims=True)
            cstat[group, 2, h : h + 1, :] = jnp.sum(p * d, axis=0, keepdims=True)

    def stat_copies(b):
        return [remote(stat.at[b], stat_in.at[b, j - 1], st_s.at[b, j - 1], st_r.at[b, j - 1], zp(j)) for j in range(1, NZ)]

    def stat_send(b):
        parts = [tuple(cstat[b * 3 + i, k] for k in range(3)) for i in range(3)]
        top = parts[0][0]
        for part in parts[1:]:
            top = jnp.maximum(top, part[0])
        total = jnp.zeros_like(top)
        dot = jnp.zeros_like(top)
        for m, l, d in parts:
            w = jnp.exp2(m - top)
            total = total + l * w
            dot = dot + d * w
        total = jnp.maximum(total, 1e-30)
        stat[b, 0] = top + jnp.log2(total)
        stat[b, 1] = dot / total
        copies = stat_copies(b)
        for j in (4, 3, 5, 2, 6, 1, 7):
            copies[j - 1].start()

    def core_copy(b):
        return remote(core_out.at[b], core_in.at[b], sc_s.at[b], sc_r.at[b], sibling)

    def merge(parts):
        top = parts[0][0]
        for part in parts[1:]:
            top = jnp.maximum(top, part[0])
        total = jnp.zeros_like(top)
        dot = jnp.zeros_like(top)
        for lse, mean in parts:
            w = jnp.exp2(lse - top)
            total = total + w
            dot = dot + mean * w
        return top + jnp.log2(total), dot / total

    def stat_ring(b):
        for copy in stat_copies(b):
            copy.wait_recv()
        parts = [(stat[b, 0], stat[b, 1])]
        parts += [(stat_in[b, j, 0], stat_in[b, j, 1]) for j in range(NZ - 1)]
        for k, value in enumerate(merge(parts)):
            core_out[b, k] = value
        core_copy(b).start()

    def stat_final(b):
        core_copy(b).wait_recv()
        lse, mean = merge([(core_out[b, 0], core_out[b, 1]), (core_in[b, 0], core_in[b, 1])])
        for i in range(3):
            alpha[b * 3 + i] = jnp.exp2(cstat[b * 3 + i, 0] - lse)
        delta[b] = mean

    def chunk_copies(i):
        r = {1: 1, 2: NX - 1, 3: 2}[i]
        return (
            remote(rs1_out.at[i - 1, 0], rs1_in.at[r - 1, 0], ra1_s.at[r - 1], ra1_r.at[r - 1], yp(r)),
            remote(rs1_out.at[i - 1, 1], rs1_in.at[r - 1, 1], rb1_s.at[r - 1], rb1_r.at[r - 1], xp(r)),
        )

    def prepare(b, i, slot, first_chunk):
        n = b * NX + i
        group = b * 3 + min(i, 1) + (i == 3)
        dqs = []
        for h in range(H):
            a = alpha[group, h : h + 1, :]
            e = delta[b, h : h + 1, :]
            p = pbuf[n, h] * a
            t = (p * (dbuf[n, h] - e)).astype(BF16)
            pb[slot][:, h * QB : (h + 1) * QB] = p.astype(BF16)
            tb[slot][:, h * QB : (h + 1) * QB] = t
            dqs.append(nn(kt[i, h * HD : (h + 1) * HD, :], t))
        dqc = jnp.concatenate(dqs, axis=0)
        dqt[b] = dqc if first_chunk else dqt[b] + dqc

    def grads(b, i, slot):
        stack_rows = slice(b * H * QB, (b + 1) * H * QB)
        dki = nn(tb[slot][...], qs[stack_rows, :])
        dvi = nn(pb[slot][...], gs[stack_rows, :])
        if b == 1:
            dki = dk[i] + dki
            dvi = dv[i] + dvi
        if b == 0 or i == 0:
            dk[i] = dki
            dv[i] = dvi
            return
        for half in range(2):
            rs1_out[i - 1, half, :, :C] = dki[half * CH : (half + 1) * CH].astype(BF16)
            rs1_out[i - 1, half, :, C:] = dvi[half * CH : (half + 1) * CH].astype(BF16)
        for copy in chunk_copies(i):
            copy.start()

    other_half = pl.ds(pl.multiple_of((1 - core) * QH, QH), QH)

    def dq_core(b):
        return remote(dq.at[b, other_half], dq_sib.at[b], dc_s.at[b], dc_r.at[b], sibling)

    def dq_start(b):
        dq[b] = dqt[b].T * SCALE
        dq_core(b).start()

    def dq_slot(b, j):
        return remote(
            dqz_out.at[b, pl.ds(j * QS, QS)],
            dqz_in.at[z],
            dz_s.at[b * NZL + j],
            dz_r.at[z],
            at(x, y, b * NZL + j, core),
        )

    def dq_ring(b):
        dq_core(b).wait_recv()
        mine = dq[b, pl.ds(pl.multiple_of(core * QH, QH), QH), :] + dq_sib[b]
        dqz_out[b] = mine.astype(BF16)
        for j in range(NZL):

            @pl.when(z == b * NZL + j)
            def _(j=j):
                dqz_own[...] = mine[j * QS : (j + 1) * QS, :]

            @pl.when(z != b * NZL + j)
            def _(j=j):
                dq_slot(b, j).start()

    head_parts = (range(H // 2), range(H // 2, H))
    first(zh, 0, 1, range(H))
    qx[0].wait_recv()
    qc[0].start()
    vx.wait_recv()
    cap_of(1 - zh)
    qc[0].wait_recv()
    stack(1 - zh, 0)
    qx[1].wait_recv()
    qc[1].start()
    first(1 - zh, 0, 1, head_parts[0])
    qc[1].wait_recv()
    stack(1 - zh, 1)
    first(1 - zh, 0, 1, head_parts[1])

    def shard(b, _):
        @pl.when(b == 0)
        def _():
            for j in (0, 2):
                for copies in (ga0, gb0, ga2, gb2):
                    copies[j].wait_recv()

        first(b, 1, 2, range(H))

        @pl.when(b == 0)
        def _():
            for copies in (ga0, gb0, ga2, gb2):
                copies[1].wait_recv()

        first(b, 3, 1, range(H))
        stat_send(b)
        return 0

    lax.fori_loop(0, NZH, shard, 0)
    for i in range(NX):
        kt[i] = kv[i * 2 * CH : (i + 1) * 2 * CH, :C].astype(F32).T.astype(BF16)
    for copy in ga0 + gb0 + ga1 + gb1 + ga2 + gb2 + qx + qc + [vx]:
        copy.wait_send()
    stat_ring(0)
    stat_final(0)
    steps = [(b, i) for b in range(NZH) for i in (3, 1, 2, 0)]
    prepare(*steps[0], 0, True)
    for k, step in enumerate(steps):
        if k == 2:
            stat_ring(1)
        if k == 3:
            stat_final(1)
        if k + 1 < len(steps):
            prepare(*steps[k + 1], (k + 1) % 2, steps[k + 1][1] == 3)
        grads(*step, k % 2)
        if k == 2:
            dq_start(0)
        if k == 4:
            dq_ring(0)
        if k == 6:
            dq_start(1)

    dq_ring(1)
    def rs2_copies(j):
        rows = pl.ds(j * KB, KB)
        return (
            remote(rs2_out.at[0, rows], rs2_in.at[j - 1, 0], ra2_s.at[j - 1], ra2_r.at[j - 1], xp(j)),
            remote(rs2_out.at[1, rows], rs2_in.at[j - 1, 1], rb2_s.at[j - 1], rb2_r.at[j - 1], yp(j)),
        )

    for half in range(2):
        for r in js:
            chunk_copies(r)[half].wait_recv()
        for part, acc in enumerate((dk, dv)):
            cols = slice(part * C, (part + 1) * C)
            total = acc[0, half * CH : (half + 1) * CH, :]
            for i in range(NX - 1):
                total = total + rs1_in[i, half, :, cols].astype(F32)
            rs2_own[half, :, cols] = total[:KB]
            rs2_out[half, :, cols] = total.astype(BF16)
        for j in (2, 1, 3):
            rs2_copies(j)[half].start()

    total = dqz_own[...]
    for j in range(1, NZ):
        sender = lax.rem(z + j, NZ)
        remote(dqz_out.at[0, pl.ds(0, QS)], dqz_in.at[sender], dz_s.at[0], dz_r.at[sender], sibling).wait_recv()
        total = total + dqz_in[sender].astype(F32)
    dqf_out[...] = total.astype(BF16)

    def dqf_copy(jz, jc):
        k = jz * NC + jc - 1
        return remote(dqf_out, dqf_in.at[k], df_s.at[k], df_r.at[k], fp(jz, jc))

    others = [(jz, jc) for jz in range(NZL) for jc in range(NC) if jz + jc > 0]
    for jz, jc in others:
        dqf_copy(jz, jc).start()
    gq_out[pl.ds(pl.multiple_of(core * QH + zl * QS, QS), QS), :] = dqf_out[...]

    for b in range(NZH):
        for copy in stat_copies(b):
            copy.wait_send()
        core_copy(b).wait_send()
        dq_core(b).wait_send()
        for j in range(NZL):

            @pl.when(z != b * NZL + j)
            def _(b=b, j=j):
                dq_slot(b, j).wait_send()

    for r in js:
        for copy in chunk_copies(r):
            copy.wait_send()
    for j in range(1, NX):
        for copy in rs2_copies(j):
            copy.wait_recv()
    for half in range(2):
        total = rs2_own[half]
        for j in range(NX - 1):
            total = total + rs2_in[j, half].astype(F32)
        gk_out[half * KB : (half + 1) * KB, :] = (total[:, :C] * SCALE).astype(BF16)
        gv_out[half * KB : (half + 1) * KB, :] = total[:, C:].astype(BF16)

    for jz, jc in others:
        dqf_copy(jz, jc).wait_recv()
        fz = lax.rem(zl - jz + NZL, NZL)
        fc = lax.rem(core - jc + NC, NC)
        gq_out[pl.ds(pl.multiple_of(fc * QH + fz * QS, QS), QS), :] = dqf_in[jz * NC + jc - 1]

    for j in js:
        for copy in rs2_copies(j):
            copy.wait_send()
    for jz, jc in others:
        dqf_copy(jz, jc).wait_send()


def write_out(a, b, c, a_out, b_out, c_out, sem):
    copies = [
        pltpu.make_async_copy(src, dst, sem.at[n])
        for n, (src, dst) in enumerate(((a, a_out), (b, b_out), (c, c_out)))
    ]
    for copy in copies:
        copy.start()
    for copy in copies:
        copy.wait()


def shards(queries, keys, values, grad_out, visible, counts):
    vmem = pl.BlockSpec(memory_space=pltpu.VMEM)
    dma = pltpu.SemaphoreType.DMA
    V = pltpu.VMEM
    blocks = NX * NZH * NY * 2
    scratch = [
        V((2, blocks), jnp.int32),
        V((1, blocks), jnp.int32),
        V((2 * CH, H * QB), BF16),
        V((2 * CH, H * QB), BF16),
        V((2 * CH, H * QB), BF16),
        V((2 * CH, H * QB), BF16),
        dma((10,)),
        V((KEYS, 2 * C), BF16),
        V((NZH, 2, 2, QB, C // 2), BF16),
        V((NZH, 8, 128), F32),
        V((NZH * H * QB, C), BF16),
        V((NZH * H * QB, C), BF16),
        V((NZH * NX, H, 2 * CH, QB), F32),
        V((NZH * NX, H, 2 * CH, QB), F32),
        V((NZH, KEYS, QB), F32),
        V((NX, C, 2 * CH), BF16),
        V((NZH * 3, 3, H, QB), F32),
        V((NZH, 2, H, QB), F32),
        V((NZH, NZ - 1, 2, H, QB), F32),
        V((NZH, 2, H, QB), F32),
        V((NZH, 2, H, QB), F32),
        V((NZH * 3, H, QB), F32),
        V((NZH, H, QB), F32),
        V((NX, 2 * CH, C), F32),
        V((NX, 2 * CH, C), F32),
        V((NX - 1, 2, CH, 2 * C), BF16),
        V((NX - 1, 2, CH, 2 * C), BF16),
        V((2, KB, 2 * C), F32),
        V((2, CH, 2 * C), BF16),
        V((NX - 1, 2, KB, 2 * C), BF16),
        V((NZH, C, QB), F32),
        V((NZH, QB, C), F32),
        V((NZH, QH, C), F32),
        V((QS, C), F32),
        V((NZH, QH, C), BF16),
        V((NZ, QS, C), BF16),
        V((QS, C), BF16),
        V((NZL * NC - 1, QS, C), BF16),
    ]
    sems = [(NX - 1,)] * 12 + [(2,)] * 6 + [(NZH, NZ - 1)] * 2 + [(NZH,)] * 2 + [(NX - 1,)] * 8
    sems += [(NZH,)] * 2 + [(NZ,)] * 2 + [(NZL * NC - 1,)] * 2
    scratch += [dma(s) for s in sems]
    shapes = [(QB, C), (2 * KB, C), (2 * KB, C)]
    anywhere = pl.BlockSpec(memory_space=pl.ANY)
    grads = pl.pallas_call(
        kernel,
        out_shape=tuple(pltpu.VMEM(s, BF16) for s in shapes),
        in_specs=[anywhere] * 6,
        out_specs=(vmem,) * 3,
        scratch_shapes=scratch,
        compiler_params=pltpu.CompilerParams(
            collective_id=0, has_side_effects=True, vmem_limit_bytes=62 * 1024 * 1024
        ),
    )(queries, grad_out, keys, values, visible, counts.reshape(1, -1))
    grads = [pltpu.with_memory_space_constraint(g, pltpu.VMEM) for g in grads]
    return pl.pallas_call(
        write_out,
        out_shape=tuple(jax.ShapeDtypeStruct(s, BF16) for s in shapes),
        in_specs=[vmem] * 3,
        out_specs=(anywhere,) * 3,
        scratch_shapes=[dma((3,))],
    )(*grads)


def solution(mesh):
    in_specs = (
        P("tile", None),
        P(("cam", "tile"), None),
        P(("cam", "tile"), None),
        P("tile", None),
        P("tile", "cam"),
        P("cam"),
    )
    out_specs = (P("tile", None), P(("cam", "tile"), None), P(("cam", "tile"), None))
    return jax.shard_map(shards, mesh=mesh, in_specs=in_specs, out_specs=out_specs, check_vma=False)
```
